32 devices in a mesh: groups: 2 (over x), tp: 8 (over z, y), sub: 2 (over core).
Axes of the slice: x: 2, y: 2, z: 4, core: 2. Of those that a mesh axis runs over, the one named last changes fastest.
Arguments:
- tokens: bfloat16 [2, 32, 16384], P(None, 'groups', ('tp', 'sub')), parts along dimension 1, may hold values from -6 to 6
- query_weight: bfloat16 [16384, 8192], P(None, ('tp', 'sub')), may hold values from -0.125 to 0.125
- key_value_weight: bfloat16 [16384, 1024], P(('tp', 'sub')), may hold values from -0.046875 to 0.046875
- output_weight: bfloat16 [8192, 16384], P(('tp', 'sub')), may hold values from -0.09375 to 0.09375
- cached_rotated_keys: bfloat16 [32, 512, 512], P(('groups', 'tp', 'sub')), parts along dimension 0, may hold values from -800 to 800, as said below
- cached_values: bfloat16 [32, 512, 512], P(('groups', 'tp', 'sub')), parts along dimension 0, may hold values from -6 to 6
- lengths: int32 [32], P(('groups', 'tp', 'sub')), parts along dimension 0, may hold values from 128 to 512, as said below
- request_adapter: int32 [32], P('groups'), parts along dimension 0, may hold values from 0 to 15
- adapter_pool_slot: int32 [16], replicated, may hold values from 0 to 15, each once
- adapter_down_maps: bfloat16 [16, 48, 16384], P(('tp', 'sub')), may hold values from -0.046875 to 0.046875
- query_up_maps: bfloat16 [16, 16, 8192], P(('tp', 'sub')), may hold values from -1.5 to 1.5
- key_up_maps: bfloat16 [16, 16, 512], P(('tp', 'sub')), may hold values from -1.5 to 1.5
- value_up_maps: bfloat16 [16, 16, 512], P(('tp', 'sub')), may hold values from -1.5 to 1.5
- result_lowering_factors: bfloat16 [16, 16, 8192], P(('tp', 'sub')), may hold values from -0.0625 to 0.0625
- output_up_maps: bfloat16 [16, 16, 16384], P(('tp', 'sub')), may hold values from -1.5 to 1.5
Outputs:
- attended: bfloat16 [2, 32, 16384], P(None, 'groups', ('tp', 'sub')), parts along dimension 1
- entries: bfloat16 [2, 32, 1024], P(None, ('groups', 'tp', 'sub')), parts along dimension 1
The draws below stay inside these ranges and needn't reach their ends.
There are 2 independent parts, one for each index of `groups`. The reference program is written for one: setup_inputs(seed, part) draws one part's arguments, and reference() takes and returns one part's arrays. A program takes and returns all parts, laid end to end along the dimension named above; an argument that names none is the same for every part. Nothing has to cross between parts.
Inputs may be any that keep to these rules, and one draw needn't show every extreme that they name: `cached_rotated_keys`: the first 64 slots of every row are filled. `lengths`: some request's cache holds exactly 512. `adapter_pool_slot`: a permutation; slot s lives on the device of index s // 1 along tp+sub.
All inputs are finite; a program needn't handle non-finite values.
Results may differ from the reference program's by a relative error of at most 0.006.
The reference program's roundings to bfloat16 on the way count: a program that leaves them out, or rounds other values in their place, can miss the bound.
Values may be sent and summed in bfloat16 or wider, within the bound.
No kernel may reach another device: no remote copies, remote signals or barrier semaphores. Data moves between devices by JAX's collectives and lax.ppermute only.
A program may use at most 128 MiB of HBM per device.

```python
import math
import jax
import jax.numpy as jnp
import numpy as np
from jax import lax

MODEL_WIDTH = 16384
ASKER_GROUPS = 64
KEY_HEADS = 4
HEAD_WIDTH = 128
ADAPTER_RANK = 16
STEPS = 2
CACHE = 512
ROWS = 16
ADAPTER_TOTAL = 16


def draw_cached_rotated_keys(key, part):
    key = jax.random.fold_in(key, 7)
    base_key = jax.random.fold_in(key, 0)
    array_shape = (ROWS, CACHE, KEY_HEADS * HEAD_WIDTH)
    values = jnp.clip(jax.random.normal(base_key, array_shape, jnp.float32), -6.0, 6.0)
    return values.astype(jnp.bfloat16)


def draw_lengths(key, part):
    key = jax.random.fold_in(key, 23)
    first_key, second_key = jax.random.split(key)
    filled = jax.random.randint(first_key, (ROWS,), CACHE // 4, CACHE + 1)
    longest = jax.random.randint(second_key, (), 0, ROWS)
    return jnp.where(jnp.arange(ROWS) == longest, CACHE, filled).astype(jnp.int32)


def with_ends(array, key, smallest, largest):
    dims = array.shape
    spot = [jax.random.randint(jax.random.fold_in(key, axis), (), 0, dims[axis]) for axis in range(len(dims))]
    array = array.at[tuple(spot)].set(smallest)
    longest = dims.index(max(dims))
    spot[longest] = (spot[longest] + 1) % dims[longest]
    return array.at[tuple(spot)].set(largest)


def with_spikes(result, key, source, target, blocks, factor):
    def block_of(axis_at):
        return (jnp.arange(result.shape[axis_at]) // (result.shape[axis_at] // blocks)).reshape((-1,) + (1,) * (result.ndim - 1 - axis_at))

    one_side = jax.random.permutation(key, blocks)[block_of(target)]
    second = (block_of(target) + blocks // 2) % blocks
    return jnp.where((block_of(source) == one_side) | (block_of(source) == second), factor * result, result)


def level_of(rng, dims, pieces, smallest, largest):
    factor_of, own = 1.0, jax.random.fold_in(rng, 6)
    for position, blocks in pieces:
        steps = jnp.exp(jax.random.uniform(jax.random.fold_in(own, position), (blocks,), jnp.float32, smallest / len(pieces), largest / len(pieces)))
        factor_of = factor_of * jnp.repeat(steps, dims[position] // blocks).reshape([-1 if axis == position else 1 for axis in range(len(dims))])
    return factor_of


def rank_table(count, skew):
    weights = [(1 << 20) // math.isqrt(rank ** skew) + 1 for rank in range(1, count + 1)]
    deviation = 1 + sum(weights) // (1 << 30)
    return np.cumsum(np.array([max(1, weight // deviation) for weight in weights]))


def ranked_ids(stream_key, shape, count, lean):
    grid = rank_table(count, lean)
    lot = jax.random.randint(jax.random.fold_in(stream_key, 1), shape, 0, int(grid[count - 1]))
    grade = jnp.searchsorted(jnp.asarray(grid, jnp.int32), lot, side="right")
    return jax.random.permutation(jax.random.fold_in(stream_key, 2), count)[grade].astype(jnp.int32)


def centred(rng, dims, deviation, limit, cuts=(), kind=jnp.bfloat16):
    values = deviation * jax.random.normal(rng, dims, jnp.float32)
    if cuts:
        values = values * level_of(rng, dims, cuts, -0.22, 0.18)
    return jnp.clip(values, -limit, limit).astype(kind)


def heavy_noise(key, shape, spread, bound, shards, heavy, kind=jnp.bfloat16):
    result = spread * jax.random.normal(key, shape, jnp.float32)
    if shards:
        result = result * level_of(key, shape, shards, -0.22, 0.18)
    return jnp.clip(with_spikes(result, jax.random.fold_in(key, 3), *heavy), -bound, bound).astype(kind)


def setup_inputs(seed: int = 0, part: int = 0) -> dict:
    streams_of = jax.random.split(jax.random.key(seed), 16)
    part_keys = jax.random.split(jax.random.fold_in(streams_of[15], part), 16)
    tokens = centred(part_keys[0], (STEPS, ROWS, MODEL_WIDTH), 1.0, 6.0, ((2, 16),))
    query_weight = centred(streams_of[1], (MODEL_WIDTH, ASKER_GROUPS * HEAD_WIDTH), (MODEL_WIDTH // 9) ** -0.5, 0.125, ((1, 16),))
    key_value_weight = centred(streams_of[2], (MODEL_WIDTH, 2 * KEY_HEADS * HEAD_WIDTH), MODEL_WIDTH ** -0.5, 0.046875, ((0, 16),))
    output_weight = heavy_noise(streams_of[3], (ASKER_GROUPS * HEAD_WIDTH, MODEL_WIDTH), (ASKER_GROUPS * HEAD_WIDTH) ** -0.5, 0.09375, ((0, 16),), (0, 1, 16, 2.0))
    cached_rotated_keys = draw_cached_rotated_keys(jax.random.fold_in(jax.random.fold_in(streams_of[15], part), 71), part)
    cached_values = centred(part_keys[5], (ROWS, CACHE, KEY_HEADS * HEAD_WIDTH), 1.0, 6.0, ((0, 16),))
    lengths = draw_lengths(jax.random.fold_in(jax.random.fold_in(streams_of[15], part), 71), part)
    request_adapter = with_ends(ranked_ids(part_keys[7], (ROWS,), ADAPTER_TOTAL, 2), jax.random.fold_in(part_keys[7], 3), 0, ADAPTER_TOTAL - 1).astype(jnp.int32)
    adapter_pool_slot = jax.random.permutation(streams_of[8], ADAPTER_TOTAL).astype(jnp.int32)
    adapter_down_maps = centred(streams_of[9], (ADAPTER_TOTAL, 3 * ADAPTER_RANK, MODEL_WIDTH), MODEL_WIDTH ** -0.5, 0.046875, ((0, 16),))
    query_up_maps = centred(streams_of[10], (ADAPTER_TOTAL, ADAPTER_RANK, ASKER_GROUPS * HEAD_WIDTH), ADAPTER_RANK ** -0.5, 1.5, ((0, 16),))
    key_up_maps = centred(streams_of[11], (ADAPTER_TOTAL, ADAPTER_RANK, KEY_HEADS * HEAD_WIDTH), ADAPTER_RANK ** -0.5, 1.5, ((0, 16),))
    value_up_maps = centred(streams_of[12], (ADAPTER_TOTAL, ADAPTER_RANK, KEY_HEADS * HEAD_WIDTH), ADAPTER_RANK ** -0.5, 1.5, ((0, 16),))
    result_lowering_factors = centred(streams_of[13], (ADAPTER_TOTAL, ADAPTER_RANK, ASKER_GROUPS * HEAD_WIDTH), (ASKER_GROUPS * HEAD_WIDTH) ** -0.5, 0.0625, ((0, 16),))
    output_up_maps = centred(streams_of[14], (ADAPTER_TOTAL, ADAPTER_RANK, MODEL_WIDTH), ADAPTER_RANK ** -0.5, 1.5, ((0, 16),))
    return dict(tokens=tokens, query_weight=query_weight, key_value_weight=key_value_weight, output_weight=output_weight, cached_rotated_keys=cached_rotated_keys, cached_values=cached_values, lengths=lengths, request_adapter=request_adapter, adapter_pool_slot=adapter_pool_slot, adapter_down_maps=adapter_down_maps, query_up_maps=query_up_maps, key_up_maps=key_up_maps, value_up_maps=value_up_maps, result_lowering_factors=result_lowering_factors, output_up_maps=output_up_maps)


adapter_scale = 0.5
rope_base = 500000.0
masked_score = -1e+30

def rotate(vectors, positions):
    half_width = vectors.shape[-1] // 2
    frequency = rope_base ** (-2.0 * jnp.arange(half_width, dtype=jnp.float32) / vectors.shape[-1])
    angles = positions.astype(jnp.float32)[..., None, None] * frequency
    cosine = jnp.cos(angles)
    sine_part = jnp.sin(angles)
    first_half = vectors[..., :half_width]
    second_half = vectors[..., half_width:]
    return jnp.concatenate([first_half * cosine - second_half * sine_part, second_half * cosine + first_half * sine_part], axis=-1)

def attend(query_rot, cached_rotated_keys, cached_values, lengths, fresh_keys, fresh_values, first_step):
    decode_iterations, row_count = (query_rot.shape[0], query_rot.shape[1])
    memory_length = cached_rotated_keys.shape[1]
    fresh_count = fresh_keys.shape[0]
    grouped = query_rot.astype(jnp.float32).reshape(decode_iterations, row_count, KEY_HEADS, ASKER_GROUPS // KEY_HEADS, HEAD_WIDTH)
    old_keys = cached_rotated_keys.astype(jnp.float32).reshape(row_count, memory_length, KEY_HEADS, HEAD_WIDTH)
    old_values = cached_values.astype(jnp.float32).reshape(row_count, memory_length, KEY_HEADS, HEAD_WIDTH)
    score_scale = 1.0 / math.sqrt(HEAD_WIDTH)
    scores_old = jnp.einsum('brkgd,rlkd->brkgl', grouped, old_keys) * score_scale
    valid_cache = jnp.arange(memory_length, dtype=jnp.int32)[None, :] < lengths[:, None]
    scores_old = jnp.where(valid_cache[None, :, None, None, :], scores_old, masked_score)
    scores_new = jnp.einsum('brkgd,trkd->brkgt', grouped, fresh_keys.astype(jnp.float32)) * score_scale
    causal = jnp.arange(fresh_count, dtype=jnp.int32)[None, :] <= first_step + jnp.arange(decode_iterations, dtype=jnp.int32)[:, None]
    scores_new = jnp.where(causal[:, None, None, None, :], scores_new, masked_score)
    highest = jnp.maximum(lax.optimization_barrier(jnp.max(scores_old, axis=-1)), lax.optimization_barrier(jnp.max(scores_new, axis=-1)))
    earlier_probabilities = jnp.exp(scores_old - highest[..., None])
    weights_new = jnp.exp(scores_new - highest[..., None])
    totals = lax.optimization_barrier(jnp.sum(earlier_probabilities, axis=-1)) + lax.optimization_barrier(jnp.sum(weights_new, axis=-1))
    probs_old = (earlier_probabilities / totals[..., None]).astype(jnp.bfloat16)
    probs_new = (weights_new / totals[..., None]).astype(jnp.bfloat16)
    attended_result_matrix = jnp.einsum('brkgl,rlkd->brkgd', probs_old.astype(jnp.float32), old_values)
    attended_result_matrix = attended_result_matrix + jnp.einsum('brkgt,trkd->brkgd', probs_new.astype(jnp.float32), fresh_values.astype(jnp.float32))
    return attended_result_matrix.reshape(decode_iterations, row_count, ASKER_GROUPS * HEAD_WIDTH).astype(jnp.bfloat16)

def reference(tokens, query_weight, key_value_weight, output_weight, cached_rotated_keys, cached_values, lengths, request_adapter, adapter_pool_slot, adapter_down_maps, query_up_maps, key_up_maps, value_up_maps, result_lowering_factors, output_up_maps):
    lender_index_entry = adapter_pool_slot[request_adapter].astype(jnp.int32)
    flat_tokens = tokens.reshape(STEPS * ROWS, MODEL_WIDTH)
    down_projected_rows = adapter_down_maps[lender_index_entry].astype(jnp.float32)
    rank_in = jnp.einsum('srd,rcd->src', tokens.astype(jnp.float32), down_projected_rows).astype(jnp.bfloat16)
    rank_as_float = rank_in.astype(jnp.float32)
    query_correction = jnp.einsum('tgj,gji->tgi', rank_as_float[..., :ADAPTER_RANK], query_up_maps[lender_index_entry].astype(jnp.float32))
    query_plain = jnp.dot(flat_tokens, query_weight, preferred_element_type=jnp.float32).reshape(STEPS, ROWS, ASKER_GROUPS * HEAD_WIDTH)
    query_head_rows = (query_plain + adapter_scale * query_correction).astype(jnp.bfloat16)
    key_value_plain = jnp.dot(flat_tokens, key_value_weight, preferred_element_type=jnp.float32).reshape(STEPS, ROWS, 2 * KEY_HEADS * HEAD_WIDTH)
    key_correction = jnp.einsum('tgj,gji->tgi', rank_as_float[..., ADAPTER_RANK:2 * ADAPTER_RANK], key_up_maps[lender_index_entry].astype(jnp.float32))
    value_correction = jnp.einsum('tgj,gji->tgi', rank_as_float[..., 2 * ADAPTER_RANK:], value_up_maps[lender_index_entry].astype(jnp.float32))
    positions = lengths[None, :] + jnp.arange(STEPS, dtype=jnp.int32)[:, None]
    unrotated_keys = key_value_plain[..., :KEY_HEADS * HEAD_WIDTH] + adapter_scale * key_correction
    keys_now = rotate(unrotated_keys.reshape(STEPS, ROWS, KEY_HEADS, HEAD_WIDTH), positions).astype(jnp.bfloat16)
    current_values = (key_value_plain[..., KEY_HEADS * HEAD_WIDTH:] + adapter_scale * value_correction).astype(jnp.bfloat16)
    query_rot = rotate(query_head_rows.astype(jnp.float32).reshape(STEPS, ROWS, ASKER_GROUPS, HEAD_WIDTH), positions).astype(jnp.bfloat16)
    attended_result_matrix = attend(query_rot, cached_rotated_keys, cached_values, lengths, keys_now, current_values.reshape(STEPS, ROWS, KEY_HEADS, HEAD_WIDTH), 0)
    output_plain = jnp.dot(attended_result_matrix.reshape(STEPS * ROWS, ASKER_GROUPS * HEAD_WIDTH), output_weight, preferred_element_type=jnp.float32).reshape(STEPS, ROWS, MODEL_WIDTH)
    result_lowered_entries = jnp.einsum('sjh,juh->sju', attended_result_matrix.astype(jnp.float32), result_lowering_factors[lender_index_entry].astype(jnp.float32)).astype(jnp.bfloat16)
    output_correction = jnp.einsum('miz,izl->mil', result_lowered_entries.astype(jnp.float32), output_up_maps[lender_index_entry].astype(jnp.float32))
    attended = (output_plain + adapter_scale * output_correction).astype(jnp.bfloat16)
    entries = jnp.concatenate([keys_now.reshape(STEPS, ROWS, KEY_HEADS * HEAD_WIDTH), current_values], axis=-1)
    return (attended, entries)
```

```python
import functools
import math

import jax
import jax.numpy as jnp
from jax import lax
from jax.experimental import pallas as pl
from jax.experimental.pallas import tpu as pltpu
from jax.sharding import PartitionSpec as P

HEAD_WIDTH = 128
ROPE_BASE = 500000.0
MASKED = -1e30
SCALE = 0.5
F32 = jnp.float32
BF16 = jnp.bfloat16

PARAMS = pltpu.CompilerParams(vmem_limit_bytes=48 * 1024 * 1024)


def nn(a, b):
    return lax.dot_general(a, b, (((1,), (0,)), ((), ())), preferred_element_type=F32)


def nt(a, b):
    return lax.dot_general(a, b, (((1,), (1,)), ((), ())), preferred_element_type=F32)


def tn(a, b):
    return lax.dot_general(a, b, (((0,), (0,)), ((), ())), preferred_element_type=F32)


def query_half_kernel(which, x_ref, w_ref, q_ref):
    @pl.when(pl.program_id(0) == 0)
    def _():
        q_ref[...] = jnp.zeros_like(q_ref)

    total = nn(x_ref[0], w_ref[0, 0])
    for j in range(1, x_ref.shape[0]):
        total = total + nn(x_ref[j], w_ref[j, 0])
    q_ref[...] += total


def query_half(which, x, weight):
    chips, rows, width = x.shape
    cols = weight.shape[-1]
    per = 2
    return pl.pallas_call(
        query_half_kernel,
        out_shape=jax.ShapeDtypeStruct((rows, cols), F32),
        grid_spec=pltpu.PrefetchScalarGridSpec(
            num_scalar_prefetch=1,
            grid=(chips // per,),
            in_specs=[
                pl.BlockSpec((per, rows, width), lambda i, s: (i, 0, 0)),
                pl.BlockSpec((per, 1, width, cols), lambda i, s: (i, s[0], 0, 0)),
            ],
            out_specs=pl.BlockSpec((rows, cols), lambda i, s: (0, 0)),
        ),
        compiler_params=PARAMS,
    )(which, x, weight)


def rank_half_kernel(which, x_ref, d_ref, r_ref):
    chips, rows, width = x_ref.shape
    total = None
    for c in range(chips):
        start = pl.multiple_of((2 * c + which[0]) * width, width)
        part = nt(d_ref[:, pl.ds(start, width)], x_ref[c])
        total = part if total is None else total + part
    r_ref[...] = total


def rank_half(which, x, down):
    return pl.pallas_call(
        rank_half_kernel,
        out_shape=jax.ShapeDtypeStruct((down.shape[0], x.shape[1]), F32),
        in_specs=[
            pl.BlockSpec(memory_space=pltpu.SMEM),
            pl.BlockSpec(memory_space=pltpu.VMEM),
            pl.BlockSpec(memory_space=pltpu.VMEM),
        ],
        compiler_params=PARAMS,
    )(which, x, down)


def dense_kernel(x_ref, w_ref, o_ref):
    o_ref[...] = nn(x_ref[...], w_ref[...])


def dense(x, weight):
    return pl.pallas_call(
        dense_kernel,
        out_shape=jax.ShapeDtypeStruct((x.shape[0], weight.shape[1]), F32),
        compiler_params=PARAMS,
    )(x, weight)


def finish_kernel(qa_ref, qb_ref, ranks_ref, mask_ref, up_ref, kv_ref, own_ref, kup_ref, vup_ref, o_ref):
    owners, rank, rows = ranks_ref.shape
    devices, steps, _ = o_ref.shape
    cols = qa_ref.shape[1]
    half = kup_ref.shape[1]
    u = ranks_ref[0].astype(F32)
    for o in range(1, owners):
        u = u + ranks_ref[o].astype(F32)
    spread = jnp.concatenate([u] * owners, axis=0) * mask_ref[...]
    query = qa_ref[...] + qb_ref[...] + SCALE * tn(spread.astype(BF16), up_ref[...])
    own = own_ref[...].astype(BF16)
    keys = kv_ref[:, :half] + SCALE * tn(own[:rank], kup_ref[...])
    values = kv_ref[:, half:] + SCALE * tn(own[rank:], vup_ref[...])
    for r in range(devices):
        for t in range(steps):
            m = t * devices + r
            o_ref[r, t : t + 1, :cols] = query[m : m + 1]
            o_ref[r, t : t + 1, cols : cols + half] = keys[m : m + 1]
            o_ref[r, t : t + 1, cols + half :] = values[m : m + 1]


def rope(v, cosine, sine):
    return v * cosine + pltpu.roll(v, HEAD_WIDTH // 2, 1) * sine


def attend_kernel(len_ref, recv_ref, cos_ref, sin_ref, k_ref, v_ref, ctx_ref, ent_ref, q_s, kn_s, vn_s):
    devices, steps, cols = ctx_ref.shape
    slots, kv_cols = k_ref.shape
    kv_heads = kv_cols // HEAD_WIDTH
    per_device = cols // HEAD_WIDTH
    group = devices * per_device // kv_heads
    rows = group * steps
    score_scale = 1.0 / math.sqrt(HEAD_WIDTH)
    length = len_ref[0]
    kv = recv_ref[0, :, cols:]
    for d in range(1, devices):
        kv = kv + recv_ref[d, :, cols:]
    cosine = cos_ref[...]
    sine = sin_ref[...]
    kn_s[...] = jnp.zeros_like(kn_s)
    vn_s[...] = jnp.zeros_like(vn_s)
    fresh = kn_s.shape[0]
    col_old = lax.broadcasted_iota(jnp.int32, (rows, slots), 1)
    col_new = lax.broadcasted_iota(jnp.int32, (rows, fresh), 1)
    step_new = lax.rem(lax.broadcasted_iota(jnp.int32, (rows, fresh), 0), steps)
    for k in range(kv_heads):
        lanes = slice(k * HEAD_WIDTH, (k + 1) * HEAD_WIDTH)
        for i in range(group):
            h = k * group + i
            d, hh = h // per_device, h % per_device
            q_s[i * steps : (i + 1) * steps, :] = recv_ref[d, :, hh * HEAD_WIDTH : (hh + 1) * HEAD_WIDTH]
        query = q_s[...].astype(BF16).astype(F32)
        query = rope(query, cosine, sine).astype(BF16)
        key_now = rope(kv[:, lanes], cosine[:steps], sine[:steps]).astype(BF16).astype(F32)
        value_now = kv[:, kv_cols + k * HEAD_WIDTH : kv_cols + (k + 1) * HEAD_WIDTH].astype(BF16).astype(F32)
        ent_ref[:, lanes] = key_now
        ent_ref[:, kv_cols + k * HEAD_WIDTH : kv_cols + (k + 1) * HEAD_WIDTH] = value_now
        kn_s[:steps, :] = key_now
        vn_s[:steps, :] = value_now
        old = nt(query, k_ref[:, lanes]) * score_scale
        old = jnp.where(col_old < length, old, MASKED)
        new = nt(query, kn_s[...].astype(BF16)) * score_scale
        new = jnp.where((col_new < steps) & (col_new <= step_new), new, MASKED)
        top = jnp.maximum(jnp.max(old, axis=1, keepdims=True), jnp.max(new, axis=1, keepdims=True))
        e_old = jnp.exp(old - top)
        e_new = jnp.exp(new - top)
        total = jnp.sum(e_old, axis=1, keepdims=True) + jnp.sum(e_new, axis=1, keepdims=True)
        p_old = (e_old / total).astype(BF16)
        p_new = (e_new / total).astype(BF16)
        out = nn(p_old, v_ref[:, lanes]) + nn(p_new, vn_s[...].astype(BF16))
        out = out.astype(BF16).astype(F32)
        for i in range(group):
            h = k * group + i
            d, hh = h // per_device, h % per_device
            ctx_ref[d, :, hh * HEAD_WIDTH : (hh + 1) * HEAD_WIDTH] = out[i * steps : (i + 1) * steps, :]


def lower_kernel(ctx_ref, mask_ref, low_ref, x_ref, part_ref, x_s):
    devices, steps, cols = ctx_ref.shape
    rank = part_ref.shape[0]
    for r in range(devices):
        for t in range(steps):
            x_s[t * devices + r : t * devices + r + 1, :] = ctx_ref[r, t : t + 1, :]
    x = x_s[...].astype(BF16)
    x_ref[...] = x
    every = nt(low_ref[...], x) * mask_ref[...]
    part = every[:rank]
    for s in range(1, every.shape[0] // rank):
        part = part + every[s * rank : (s + 1) * rank]
    part_ref[...] = part


def out_half_kernel(which, x_ref, w_ref, o_ref):
    o_ref[0] = nn(x_ref[...], w_ref[...])


def out_half(which, x, weight, chips):
    rows, cols = x.shape
    width = weight.shape[1] // (2 * chips)
    return pl.pallas_call(
        out_half_kernel,
        out_shape=jax.ShapeDtypeStruct((chips, rows, width), F32),
        grid_spec=pltpu.PrefetchScalarGridSpec(
            num_scalar_prefetch=1,
            grid=(chips,),
            in_specs=[
                pl.BlockSpec((rows, cols), lambda i, s: (0, 0)),
                pl.BlockSpec((cols, width), lambda i, s: (0, 2 * i + s[0])),
            ],
            out_specs=pl.BlockSpec((1, rows, width), lambda i, s: (i, 0, 0)),
        ),
        compiler_params=PARAMS,
    )(which, x, weight)


def pair_kernel(a_ref, b_ref, parts_ref, mask_ref, up_ref, o_ref):
    u = parts_ref[0]
    for d in range(1, parts_ref.shape[0]):
        u = u + parts_ref[d]
    u = u.astype(BF16).astype(F32)
    spread = jnp.concatenate([u * mask_ref[0:1, :], u * mask_ref[1:2, :]], axis=0).astype(BF16)
    for c in range(a_ref.shape[0]):
        o_ref[c] = (a_ref[c] + b_ref[c] + SCALE * tn(spread, up_ref[c])).astype(BF16)


def total_kernel(x_ref, o_ref):
    total = x_ref[0].astype(F32)
    for c in range(1, x_ref.shape[0]):
        total = total + x_ref[c].astype(F32)
    o_ref[...] = total.astype(BF16)


def body(
    tokens,
    query_weight,
    key_value_weight,
    output_weight,
    cached_rotated_keys,
    cached_values,
    lengths,
    request_adapter,
    adapter_pool_slot,
    adapter_down_maps,
    query_up_maps,
    key_up_maps,
    value_up_maps,
    result_lowering_factors,
    output_up_maps,
):
    both = ("tp", "sub")
    chips = lax.axis_size("tp")
    devices = lax.axis_size(both)
    me = lax.axis_index(both)
    core = lax.axis_index("sub")
    steps, requests, width = tokens.shape
    rows = steps * requests
    cols = query_weight.shape[1]
    rank = key_up_maps.shape[1]
    pool = devices
    assert adapter_down_maps.shape[0] == 1 and requests == devices and cached_values.shape[0] == 1
    swap = [(0, 1), (1, 0)]
    here = core.astype(jnp.int32).reshape(1)
    there = 1 - here

    x = tokens.reshape(rows, width)
    copies = jnp.broadcast_to(x[None], (chips, rows, width))
    mine = lax.all_to_all(copies, "tp", 0, 0, tiled=True)
    other = lax.ppermute(mine, "sub", swap)

    kv = dense(x, key_value_weight)

    index = jnp.arange(pool, dtype=jnp.int32)
    slot = jnp.sum(
        jnp.where(request_adapter[:, None] == index[None, :], adapter_pool_slot[None, :], 0), axis=1
    )
    row_slot = jnp.tile(slot, steps)[None, :]
    spread_mask = (jnp.repeat(index, rank)[:, None] == row_slot).astype(F32)
    own_mask = (row_slot == me).astype(F32)
    pair_mask = (jnp.stack([me, me + 1 - 2 * core])[:, None] == row_slot).astype(F32)

    def by_heads(maps, after):
        pieces = maps.reshape(rank, devices, cols).transpose(1, 0, 2)
        pieces, _ = lax.optimization_barrier((pieces, after))
        return lax.all_to_all(pieces, both, 0, 0, tiled=True).reshape(pool * rank, cols)

    up_by_heads = by_heads(query_up_maps, mine)

    out_up = output_up_maps.reshape(rank, chips, 2, width).transpose(2, 1, 0, 3)
    up_here = lax.dynamic_index_in_dim(out_up, core, 0, keepdims=False)
    up_there = lax.dynamic_index_in_dim(out_up, 1 - core, 0, keepdims=False)
    up_pair = jnp.concatenate([up_here, lax.ppermute(up_there, "sub", swap)], axis=1)

    down = adapter_down_maps.reshape(adapter_down_maps.shape[1], -1)
    weight = query_weight.reshape(chips, 2, width, cols)
    q_mine = query_half(here, mine, weight)
    rank_mine = rank_half(here, mine, down)
    rank_all = (rank_mine + rank_half(there, other, down)).astype(BF16).astype(F32) * own_mask
    rank_query = rank_all[:rank].astype(BF16)
    ranks = lax.all_to_all(
        jnp.broadcast_to(rank_query[None], (devices, rank, rows)), both, 0, 0, tiled=True
    )
    q_other = query_half(there, other, weight)
    to_rows = pl.pallas_call(
        finish_kernel,
        out_shape=jax.ShapeDtypeStruct((devices, steps, cols + kv.shape[1]), F32),
        compiler_params=PARAMS,
    )(
        q_mine,
        q_other,
        ranks,
        spread_mask,
        up_by_heads,
        kv,
        rank_all[rank:],
        key_up_maps[0],
        value_up_maps[0],
    )
    arrived = lax.all_to_all(to_rows, both, 0, 0, tiled=True)

    low_by_heads = by_heads(result_lowering_factors, arrived)

    kv_cols = key_value_weight.shape[1] // 2
    half_width = HEAD_WIDTH // 2
    frequency = ROPE_BASE ** (-2.0 * jnp.arange(half_width, dtype=F32) / HEAD_WIDTH)
    positions = lengths[0] + jnp.arange(steps, dtype=jnp.int32)
    angles = positions.astype(F32)[:, None] * frequency
    cosine, sine = jnp.cos(angles), jnp.sin(angles)
    group = devices * cols // kv_cols
    cosine = jnp.tile(jnp.concatenate([cosine, cosine], axis=1), (group, 1))
    sine = jnp.tile(jnp.concatenate([-sine, sine], axis=1), (group, 1))
    vmem = pl.BlockSpec(memory_space=pltpu.VMEM)
    context, fresh = pl.pallas_call(
        attend_kernel,
        out_shape=(
            jax.ShapeDtypeStruct((devices, steps, cols), F32),
            jax.ShapeDtypeStruct((steps, 2 * kv_cols), F32),
        ),
        in_specs=[pl.BlockSpec(memory_space=pltpu.SMEM)] + [vmem] * 5,
        scratch_shapes=[
            pltpu.VMEM((group * steps, HEAD_WIDTH), F32),
            pltpu.VMEM((16, HEAD_WIDTH), F32),
            pltpu.VMEM((16, HEAD_WIDTH), F32),
        ],
        compiler_params=PARAMS,
    )(lengths, arrived, cosine, sine, cached_rotated_keys[0], cached_values[0])
    entries = fresh.astype(BF16)[:, None, :]

    by_head = lax.all_to_all(context, both, 0, 0, tiled=True)
    lhs, part = pl.pallas_call(
        lower_kernel,
        out_shape=(
            jax.ShapeDtypeStruct((rows, cols), BF16),
            jax.ShapeDtypeStruct((rank, rows), F32),
        ),
        scratch_shapes=[pltpu.VMEM((rows, cols), F32)],
        compiler_params=PARAMS,
    )(by_head, spread_mask, low_by_heads)
    parts = lax.all_to_all(
        jnp.broadcast_to(part[None], (devices, rank, rows)), both, 0, 0, tiled=True
    )
    out_there = out_half(there, lhs, output_weight, chips)
    received = lax.ppermute(out_there, "sub", swap)
    out_here = out_half(here, lhs, output_weight, chips)
    chip_total = pl.pallas_call(
        pair_kernel,
        out_shape=jax.ShapeDtypeStruct((chips, rows, width), BF16),
        compiler_params=PARAMS,
    )(out_here, received, parts, pair_mask, up_pair)
    pieces = lax.all_to_all(chip_total, "tp", 0, 0, tiled=True)
    attended = pl.pallas_call(
        total_kernel,
        out_shape=jax.ShapeDtypeStruct((rows, width), BF16),
        compiler_params=PARAMS,
    )(pieces)
    return attended.reshape(steps, requests, width), entries


def solution(mesh):
    placed = (
        P(None, "groups", ("tp", "sub")),
        P(None, ("tp", "sub")),
        P(("tp", "sub"), None),
        P(("tp", "sub"), None),
        P(("groups", "tp", "sub"), None, None),
        P(("groups", "tp", "sub"), None, None),
        P(("groups", "tp", "sub")),
        P("groups"),
        P(),
        P(("tp", "sub"), None, None),
        P(("tp", "sub"), None, None),
        P(("tp", "sub"), None, None),
        P(("tp", "sub"), None, None),
        P(("tp", "sub"), None, None),
        P(("tp", "sub"), None, None),
    )
    return jax.shard_map(
        body,
        mesh=mesh,
        in_specs=placed,
        out_specs=(P(None, "groups", ("tp", "sub")), P(None, ("groups", "tp", "sub"), None)),
        check_vma=False,
    )
```

```python
import functools
import math

import jax
import jax.numpy as jnp
from jax import lax
from jax.experimental import pallas as pl
from jax.experimental.pallas import tpu as pltpu
from jax.sharding import PartitionSpec as P

HEAD_WIDTH = 128
ROPE_BASE = 500000.0
MASKED = -1e30
SCALE = 0.5
F32 = jnp.float32
BF16 = jnp.bfloat16

PARAMS = pltpu.CompilerParams(vmem_limit_bytes=16 * 1024 * 1024)


def nn(a, b):
    return lax.dot_general(a, b, (((1,), (0,)), ((), ())), preferred_element_type=F32)


def nt(a, b):
    return lax.dot_general(a, b, (((1,), (1,)), ((), ())), preferred_element_type=F32)


def tn(a, b):
    return lax.dot_general(a, b, (((0,), (0,)), ((), ())), preferred_element_type=F32)


VMEM = pl.BlockSpec(memory_space=pltpu.VMEM)
SMEM = pl.BlockSpec(memory_space=pltpu.SMEM)
ANY = pl.BlockSpec(memory_space=pl.ANY)


def device_at(at_ref, chips, k, sign):
    dt, ds = k // 2, k % 2
    tp = lax.rem(at_ref[0] + chips + sign * dt, chips)
    core = at_ref[1] if ds == 0 else 1 - at_ref[1]
    return 2 * tp + core


def chip_at(at_ref, chips, k, flip):
    lines = chips // 2
    z = lax.rem(at_ref[0] // 2 + lines - k, lines)
    y = lax.rem(at_ref[0], 2)
    return 2 * z + (1 - y if flip else y)


def piece_at(at_ref, chips, k, flip, cross):
    core = 1 - at_ref[1] if cross else at_ref[1]
    return 2 * chip_at(at_ref, chips, k, flip) + core


def query_kernel(flip, cross, chips, *refs):
    at_ref, w_ref = refs[0], refs[1]
    pieces = refs[2:-3]
    q_ref, w_s, sems = refs[-3:]
    width = pieces[0].shape[1]
    copies = []
    for k in range(len(pieces)):
        start = pl.multiple_of(piece_at(at_ref, chips, k, flip, cross) * width, width)
        copy = pltpu.make_async_copy(w_ref.at[pl.ds(start, width)], w_s.at[k], sems.at[k])
        copy.start()
        copies.append(copy)
    total = None
    for k, piece in enumerate(pieces):
        copies[k].wait()
        part = nn(piece[...], w_s[k])
        total = part if total is None else total + part
    q_ref[...] = total


def query_pieces(at, weight, pieces, chips, flip, cross):
    rows, width = pieces[0].shape
    cols = weight.shape[1]
    return pl.pallas_call(
        functools.partial(query_kernel, flip, cross, chips),
        out_shape=jax.ShapeDtypeStruct((rows, cols), F32),
        in_specs=[SMEM, ANY] + [VMEM] * len(pieces),
        scratch_shapes=[
            pltpu.VMEM((len(pieces), width, cols), BF16),
            pltpu.SemaphoreType.DMA((len(pieces),)),
        ],
        compiler_params=PARAMS,
    )(at, weight, *pieces)


def rank_kernel(kinds, chips, *refs):
    at_ref, d_ref = refs[0], refs[1]
    pieces, r_ref = refs[2:-1], refs[-1]
    width = pieces[0].shape[1]
    total = None
    for (k, flip, cross), piece in zip(kinds, pieces):
        start = pl.multiple_of(piece_at(at_ref, chips, k, flip, cross) * width, width)
        part = nt(d_ref[:, pl.ds(start, width)], piece[...])
        total = part if total is None else total + part
    r_ref[...] = total


def rank_pieces(at, down, pieces, kinds, chips):
    return pl.pallas_call(
        functools.partial(rank_kernel, kinds, chips),
        out_shape=jax.ShapeDtypeStruct((down.shape[0], pieces[0].shape[0]), F32),
        in_specs=[SMEM] + [VMEM] * (1 + len(pieces)),
        compiler_params=PARAMS,
    )(at, down, *pieces)


def dense_kernel(x_ref, w_ref, o_ref):
    o_ref[...] = nn(x_ref[...], w_ref[...])


def dense(x, weight):
    return pl.pallas_call(
        dense_kernel,
        out_shape=jax.ShapeDtypeStruct((x.shape[0], weight.shape[1]), F32),
        compiler_params=PARAMS,
    )(x, weight)


def split_kernel(chips, at_ref, m_ref, dep_ref, *outs):
    cols = outs[0].shape[1]
    for k, out in enumerate(outs):
        start = pl.multiple_of(device_at(at_ref, chips, k, 1) * cols, cols)
        out[...] = m_ref[:, pl.ds(start, cols)]


def split_map(at, maps, dep, chips):
    rank, width = maps.shape
    devices = 2 * chips
    return pl.pallas_call(
        functools.partial(split_kernel, chips),
        out_shape=[jax.ShapeDtypeStruct((rank, width // devices), BF16)] * devices,
        in_specs=[SMEM, VMEM, ANY],
        compiler_params=PARAMS,
    )(at, maps, dep)


def other_half_kernel(at_ref, m_ref, o_ref):
    width = o_ref.shape[2]
    for c in range(o_ref.shape[0]):
        start = pl.multiple_of((2 * c + 1 - at_ref[1]) * width, width)
        o_ref[c] = m_ref[:, pl.ds(start, width)]


def finish_kernel(chips, *refs):
    devices = 2 * chips
    at_ref, mask_ref, own_ref, kv_ref, kup_ref, vup_ref = refs[:6]
    rest = refs[6:]
    ups, rest = rest[:devices], rest[devices:]
    ranks, rest = rest[:devices], rest[devices:]
    queries, rest = rest[: -devices - 1], rest[-devices - 1 :]
    outs, y_s = rest[:devices], rest[devices]
    rank = ranks[0].shape[0]
    cols = queries[0].shape[1]
    half = kup_ref.shape[1]
    steps = outs[0].shape[0]
    u = ranks[0][...].astype(F32)
    for r in ranks[1:]:
        u = u + r[...].astype(F32)
    query = queries[0][...]
    for q in queries[1:]:
        query = query + q[...]
    spread = []
    for k in range(devices):
        start = pl.multiple_of(device_at(at_ref, chips, k, -1) * rank, rank)
        spread.append(u * mask_ref[pl.ds(start, rank), :])
    spread = jnp.concatenate(spread, axis=0).astype(BF16)
    up = jnp.concatenate([m[...] for m in ups], axis=0)
    y_s[:, :cols] = query + SCALE * tn(spread, up)
    own = own_ref[...].astype(BF16)
    y_s[:, cols : cols + half] = kv_ref[:, :half] + SCALE * tn(own[:rank], kup_ref[...])
    y_s[:, cols + half :] = kv_ref[:, half:] + SCALE * tn(own[rank:], vup_ref[...])
    for k, out in enumerate(outs):
        dest = device_at(at_ref, chips, k, 1)
        for t in range(steps):
            out[t : t + 1, :] = y_s[pl.ds(t * devices + dest, 1), :]


def rope(v, cosine, sine):
    return v * cosine + pltpu.roll(v, HEAD_WIDTH // 2, 1) * sine


def attend_kernel(chips, *refs):
    devices = 2 * chips
    at_ref, len_ref, cos_ref, sin_ref, k_ref, v_ref = refs[:6]
    rest = refs[6:]
    arrived, rest = rest[:devices], rest[devices:]
    outs, rest = rest[:devices], rest[devices:]
    ent_ref, q_s, c_s, kn_s, vn_s = rest
    steps, cols = outs[0].shape
    slots, kv_cols = k_ref.shape
    kv_heads = kv_cols // HEAD_WIDTH
    per_device = cols // HEAD_WIDTH
    group = devices * per_device // kv_heads
    rows = group * steps
    score_scale = 1.0 / math.sqrt(HEAD_WIDTH)
    length = len_ref[0]
    kv = arrived[0][:, cols:]
    for a in arrived[1:]:
        kv = kv + a[:, cols:]
    for k, a in enumerate(arrived):
        first = device_at(at_ref, chips, k, -1) * (per_device * steps)
        for hh in range(per_device):
            for t in range(steps):
                q_s[pl.ds(first + hh * steps + t, 1), :] = a[t : t + 1, hh * HEAD_WIDTH : (hh + 1) * HEAD_WIDTH]
    cosine = cos_ref[...]
    sine = sin_ref[...]
    kn_s[...] = jnp.zeros_like(kn_s)
    vn_s[...] = jnp.zeros_like(vn_s)
    fresh = kn_s.shape[0]
    col_old = lax.broadcasted_iota(jnp.int32, (rows, slots), 1)
    col_new = lax.broadcasted_iota(jnp.int32, (rows, fresh), 1)
    step_new = lax.rem(lax.broadcasted_iota(jnp.int32, (rows, fresh), 0), steps)
    for k in range(kv_heads):
        lanes = slice(k * HEAD_WIDTH, (k + 1) * HEAD_WIDTH)
        value_lanes = slice(kv_cols + k * HEAD_WIDTH, kv_cols + (k + 1) * HEAD_WIDTH)
        query = q_s[k * rows : (k + 1) * rows, :].astype(BF16).astype(F32)
        query = rope(query, cosine, sine).astype(BF16)
        key_now = rope(kv[:, lanes], cosine[:steps], sine[:steps]).astype(BF16).astype(F32)
        value_now = kv[:, value_lanes].astype(BF16).astype(F32)
        ent_ref[:, lanes] = key_now
        ent_ref[:, value_lanes] = value_now
        kn_s[:steps, :] = key_now
        vn_s[:steps, :] = value_now
        old = nt(query, k_ref[:, lanes]) * score_scale
        old = jnp.where(col_old < length, old, MASKED)
        new = nt(query, kn_s[...].astype(BF16)) * score_scale
        new = jnp.where((col_new < steps) & (col_new <= step_new), new, MASKED)
        top = jnp.maximum(jnp.max(old, axis=1, keepdims=True), jnp.max(new, axis=1, keepdims=True))
        e_old = jnp.exp(old - top)
        e_new = jnp.exp(new - top)
        total = jnp.sum(e_old, axis=1, keepdims=True) + jnp.sum(e_new, axis=1, keepdims=True)
        p_old = (e_old / total).astype(BF16)
        p_new = (e_new / total).astype(BF16)
        out = nn(p_old, v_ref[:, lanes]) + nn(p_new, vn_s[...].astype(BF16))
        c_s[k * rows : (k + 1) * rows, :] = out.astype(BF16).astype(F32)
    for k, out in enumerate(outs):
        first = device_at(at_ref, chips, k, 1) * (per_device * steps)
        for hh in range(per_device):
            for t in range(steps):
                out[t : t + 1, hh * HEAD_WIDTH : (hh + 1) * HEAD_WIDTH] = c_s[pl.ds(first + hh * steps + t, 1), :]


def lower_kernel(chips, *refs):
    devices = 2 * chips
    at_ref, mask_ref = refs[:2]
    rest = refs[2:]
    lows, rest = rest[:devices], rest[devices:]
    arrived, rest = rest[:devices], rest[devices:]
    x_ref, part_ref, x_s = rest
    steps = arrived[0].shape[0]
    rank = part_ref.shape[0]
    for k, a in enumerate(arrived):
        source = device_at(at_ref, chips, k, -1)
        for t in range(steps):
            x_s[pl.ds(t * devices + source, 1), :] = a[t : t + 1, :]
    x = x_s[...].astype(BF16)
    x_ref[...] = x
    every = nt(jnp.concatenate([m[...] for m in lows], axis=0), x)
    part = None
    for k in range(devices):
        start = pl.multiple_of(device_at(at_ref, chips, k, -1) * rank, rank)
        one = every[k * rank : (k + 1) * rank] * mask_ref[pl.ds(start, rank), :]
        part = one if part is None else part + one
    part_ref[...] = part


def out_half_kernel(cross, at_ref, x_ref, w_ref, o_ref):
    width = o_ref.shape[2]
    core = 1 - at_ref[1] if cross else at_ref[1]
    x = x_ref[...]
    for c in range(o_ref.shape[0]):
        start = pl.multiple_of((2 * c + core) * width, width)
        o_ref[c] = nn(x, w_ref[:, pl.ds(start, width)])


def out_half(at, x, weight, chips, cross):
    width = weight.shape[1] // (2 * chips)
    return pl.pallas_call(
        functools.partial(out_half_kernel, cross),
        out_shape=jax.ShapeDtypeStruct((chips, x.shape[0], width), F32),
        in_specs=[SMEM, VMEM, VMEM],
        compiler_params=PARAMS,
    )(at, x, weight)


def pair_kernel(chips, *refs):
    devices = 2 * chips
    at_ref, a_ref, b_ref, mask_ref, up_ref, other_ref = refs[:6]
    parts, outs = refs[6 : 6 + devices], refs[6 + devices :]
    width = outs[0].shape[1]
    u = parts[0][...]
    for p in parts[1:]:
        u = u + p[...]
    u = u.astype(BF16).astype(F32)
    spread = jnp.concatenate([u * mask_ref[0:1, :], u * mask_ref[1:2, :]], axis=0).astype(BF16)
    for k, out in enumerate(outs):
        dest = lax.rem(at_ref[0] + k, chips)
        start = pl.multiple_of((2 * dest + at_ref[1]) * width, width)
        up = jnp.concatenate([up_ref[:, pl.ds(start, width)], other_ref[dest]], axis=0)
        out[...] = (a_ref[dest] + b_ref[dest] + SCALE * tn(spread, up)).astype(BF16)


def total_kernel(*refs):
    total = refs[0][...].astype(F32)
    for r in refs[1:-1]:
        total = total + r[...].astype(F32)
    refs[-1][...] = total.astype(BF16)


def body(
    tokens,
    query_weight,
    key_value_weight,
    output_weight,
    cached_rotated_keys,
    cached_values,
    lengths,
    request_adapter,
    adapter_pool_slot,
    adapter_down_maps,
    query_up_maps,
    key_up_maps,
    value_up_maps,
    result_lowering_factors,
    output_up_maps,
):
    both = ("tp", "sub")
    chips = lax.axis_size("tp")
    devices = lax.axis_size(both)
    lines = chips // 2
    me = lax.axis_index(both)
    core = lax.axis_index("sub")
    steps, requests, width = tokens.shape
    rows = steps * requests
    cols = query_weight.shape[1]
    rank = key_up_maps.shape[1]
    assert devices == 2 * chips and chips % 2 == 0
    assert adapter_down_maps.shape[0] == 1 and requests == devices and cached_values.shape[0] == 1
    at = jnp.stack([lax.axis_index("tp"), core]).astype(jnp.int32)

    def swap_core(v):
        return lax.ppermute(v, "sub", [(0, 1), (1, 0)])

    def swap_y(v):
        return lax.ppermute(v, "tp", [(i, i ^ 1) for i in range(chips)])

    def shift_z(v, k):
        return lax.ppermute(v, "tp", [(i, (i + 2 * k) % chips) for i in range(chips)])

    def shift(v, k):
        if k == 0:
            return v
        return lax.ppermute(
            v, both, [(i, (i // 2 + k // 2) % chips * 2 + (i % 2 ^ k % 2)) for i in range(devices)]
        )

    few = devices <= 16
    places = jnp.arange(devices, dtype=jnp.int32)

    def place(sign):
        return (at[0] + sign * (places // 2)) % chips * 2 + (core ^ places % 2)

    def exchange(pieces):
        if few:
            return [shift(v, k) for k, v in enumerate(pieces)]
        stacked = jnp.stack(pieces)
        sent = jnp.zeros_like(stacked).at[place(1)].set(stacked)
        return list(lax.all_to_all(sent, both, 0, 0, tiled=True)[place(-1)])

    def spread_all(v):
        if few:
            return [shift(v, k) for k in range(devices)]
        return list(lax.all_gather(v, both)[place(-1)])

    x = tokens.reshape(rows, width)
    line = [x] + [shift_z(x, k) for k in range(1, lines)]
    across = [swap_y(v) for v in line]
    line_cross = [swap_core(v) for v in line]
    across_cross = [swap_core(v) for v in across]

    kv = dense(x, key_value_weight)

    index = jnp.arange(devices, dtype=jnp.int32)
    slot = jnp.sum(
        jnp.where(request_adapter[:, None] == index[None, :], adapter_pool_slot[None, :], 0), axis=1
    )
    row_slot = jnp.tile(slot, steps)[None, :]
    spread_mask = (jnp.repeat(index, rank)[:, None] == row_slot).astype(F32)
    own_mask = (row_slot == me).astype(F32)
    pair_mask = (jnp.stack([me, me + 1 - 2 * core])[:, None] == row_slot).astype(F32)

    ups = exchange(split_map(at, query_up_maps[0], line[-1], chips))

    up_other = swap_core(
        pl.pallas_call(
            other_half_kernel,
            out_shape=jax.ShapeDtypeStruct((chips, rank, width), BF16),
            in_specs=[SMEM, VMEM],
            compiler_params=PARAMS,
        )(at, output_up_maps[0])
    )

    down = adapter_down_maps[0]
    order = range(lines)
    early = rank_pieces(
        at,
        down,
        line + across + line_cross,
        [(k, False, False) for k in order] + [(k, True, False) for k in order] + [(k, False, True) for k in order],
        chips,
    )
    late = rank_pieces(at, down, across_cross, [(k, True, True) for k in order], chips)
    rank_all = (early + late).astype(BF16).astype(F32) * own_mask
    ranks = spread_all(rank_all[:rank].astype(BF16))
    queries = [
        query_pieces(at, query_weight, line, chips, False, False),
        query_pieces(at, query_weight, across, chips, True, False),
        query_pieces(at, query_weight, line_cross, chips, False, True),
        query_pieces(at, query_weight, across_cross, chips, True, True),
    ]
    to_rows = pl.pallas_call(
        functools.partial(finish_kernel, chips),
        out_shape=[jax.ShapeDtypeStruct((steps, cols + kv.shape[1]), F32)] * devices,
        in_specs=[SMEM] + [VMEM] * (5 + 2 * devices + len(queries)),
        scratch_shapes=[pltpu.VMEM((rows, cols + kv.shape[1]), F32)],
        compiler_params=PARAMS,
    )(at, spread_mask, rank_all[rank:], kv, key_up_maps[0], value_up_maps[0], *ups, *ranks, *queries)
    arrived = exchange(to_rows)

    lows = exchange(split_map(at, result_lowering_factors[0], ranks[-1], chips))

    kv_cols = key_value_weight.shape[1] // 2
    half_width = HEAD_WIDTH // 2
    frequency = ROPE_BASE ** (-2.0 * jnp.arange(half_width, dtype=F32) / HEAD_WIDTH)
    positions = lengths[0] + jnp.arange(steps, dtype=jnp.int32)
    angles = positions.astype(F32)[:, None] * frequency
    cosine, sine = jnp.cos(angles), jnp.sin(angles)
    heads = devices * cols // HEAD_WIDTH
    group = devices * cols // kv_cols
    cosine = jnp.tile(jnp.concatenate([cosine, cosine], axis=1), (group, 1))
    sine = jnp.tile(jnp.concatenate([-sine, sine], axis=1), (group, 1))
    results = pl.pallas_call(
        functools.partial(attend_kernel, chips),
        out_shape=[jax.ShapeDtypeStruct((steps, cols), F32)] * devices
        + [jax.ShapeDtypeStruct((steps, 2 * kv_cols), F32)],
        in_specs=[SMEM, SMEM] + [VMEM] * (4 + devices),
        scratch_shapes=[
            pltpu.VMEM((heads * steps, HEAD_WIDTH), F32),
            pltpu.VMEM((heads * steps, HEAD_WIDTH), F32),
            pltpu.VMEM((16, HEAD_WIDTH), F32),
            pltpu.VMEM((16, HEAD_WIDTH), F32),
        ],
        compiler_params=PARAMS,
    )(at, lengths, cosine, sine, cached_rotated_keys[0], cached_values[0], *arrived)
    entries = results[-1].astype(BF16)[:, None, :]

    by_head = exchange(results[:-1])
    lhs, part = pl.pallas_call(
        functools.partial(lower_kernel, chips),
        out_shape=(
            jax.ShapeDtypeStruct((rows, cols), BF16),
            jax.ShapeDtypeStruct((rank, rows), F32),
        ),
        in_specs=[SMEM] + [VMEM] * (1 + 2 * devices),
        scratch_shapes=[pltpu.VMEM((rows, cols), F32)],
        compiler_params=PARAMS,
    )(at, spread_mask, *lows, *by_head)
    parts = spread_all(part)
    out_there = out_half(at, lhs, output_weight, chips, True)
    received = swap_core(out_there)
    out_here = out_half(at, lhs, output_weight, chips, False)
    chip_totals = pl.pallas_call(
        functools.partial(pair_kernel, chips),
        out_shape=[jax.ShapeDtypeStruct((rows, width), BF16)] * chips,
        in_specs=[SMEM] + [VMEM] * (5 + devices),
        compiler_params=PARAMS,
    )(at, out_here, received, pair_mask, output_up_maps[0], up_other, *parts)
    pieces = [shift(v, 2 * k) for k, v in enumerate(chip_totals)]
    attended = pl.pallas_call(
        total_kernel,
        out_shape=jax.ShapeDtypeStruct((rows, width), BF16),
        compiler_params=PARAMS,
    )(*pieces)
    return attended.reshape(steps, requests, width), entries


def solution(mesh):
    placed = (
        P(None, "groups", ("tp", "sub")),
        P(None, ("tp", "sub")),
        P(("tp", "sub"), None),
        P(("tp", "sub"), None),
        P(("groups", "tp", "sub"), None, None),
        P(("groups", "tp", "sub"), None, None),
        P(("groups", "tp", "sub")),
        P("groups"),
        P(),
        P(("tp", "sub"), None, None),
        P(("tp", "sub"), None, None),
        P(("tp", "sub"), None, None),
        P(("tp", "sub"), None, None),
        P(("tp", "sub"), None, None),
        P(("tp", "sub"), None, None),
    )
    return jax.shard_map(
        body,
        mesh=mesh,
        in_specs=placed,
        out_specs=(P(None, "groups", ("tp", "sub")), P(None, ("groups", "tp", "sub"), None)),
        check_vma=False,
    )
```

```python
import functools
import math

import jax
import jax.numpy as jnp
from jax import lax
from jax.experimental import pallas as pl
from jax.experimental.pallas import tpu as pltpu
from jax.sharding import PartitionSpec as P

HEAD_WIDTH = 128
ROPE_BASE = 500000.0
MASKED = -1e30
SCALE = 0.5
F32 = jnp.float32
BF16 = jnp.bfloat16

PARAMS = pltpu.CompilerParams(vmem_limit_bytes=16 * 1024 * 1024)


def nn(a, b):
    return lax.dot_general(a, b, (((1,), (0,)), ((), ())), preferred_element_type=F32)


def nt(a, b):
    return lax.dot_general(a, b, (((1,), (1,)), ((), ())), preferred_element_type=F32)


def tn(a, b):
    return lax.dot_general(a, b, (((0,), (0,)), ((), ())), preferred_element_type=F32)


WIDE = pltpu.CompilerParams(vmem_limit_bytes=52 * 1024 * 1024)
VMEM = pl.BlockSpec(memory_space=pltpu.VMEM)
SMEM = pl.BlockSpec(memory_space=pltpu.SMEM)
HBM = pl.BlockSpec(memory_space=pltpu.HBM)
ANY = pl.BlockSpec(memory_space=pl.ANY)


def piece_at(at_ref, chips, k, flip, cross):
    lines = chips // 2
    z = lax.rem(at_ref[0] // 2 + lines - k, lines)
    y = lax.rem(at_ref[0], 2)
    core = 1 - at_ref[1] if cross else at_ref[1]
    return 4 * z + 2 * (1 - y if flip else y) + core


def stack_kernel(*refs):
    for k, r in enumerate(refs[:-1]):
        refs[-1][k] = r[...]


def query_kernel(flip, cross, *refs):
    at_ref, w_ref, x_ref = refs[:3]
    q_ref, w_s, sems = refs[-3:]
    lines, _, width = x_ref.shape
    copies = []
    for k in range(lines):
        start = pl.multiple_of(piece_at(at_ref, 2 * lines, k, flip, cross) * width, width)
        copy = pltpu.make_async_copy(w_ref.at[pl.ds(start, width)], w_s.at[k], sems.at[k])
        copy.start()
        copies.append(copy)
    total = refs[3][...] if len(refs) > 6 else None
    for k in range(lines):
        copies[k].wait()
        part = nn(x_ref[k], w_s[k])
        total = part if total is None else total + part
    q_ref[...] = total


def query_stack(at, weight, x, flip, cross, *before):
    lines, rows, width = x.shape
    cols = weight.shape[1]
    return pl.pallas_call(
        functools.partial(query_kernel, flip, cross),
        out_shape=jax.ShapeDtypeStruct((rows, cols), F32),
        in_specs=[SMEM, HBM] + [VMEM] * (1 + len(before)),
        scratch_shapes=[
            pltpu.VMEM((lines, width, cols), BF16),
            pltpu.SemaphoreType.DMA((lines,)),
        ],
        compiler_params=WIDE,
    )(at, weight, x, *before)


def rank_sum(at_ref, d_ref, stacks, kinds, total):
    for x_ref, (flip, cross) in zip(stacks, kinds):
        lines, _, width = x_ref.shape
        for k in range(lines):
            start = pl.multiple_of(piece_at(at_ref, 2 * lines, k, flip, cross) * width, width)
            part = nt(d_ref[:, pl.ds(start, width)], x_ref[k])
            total = part if total is None else total + part
    return total


def rank_early_kernel(at_ref, d_ref, a_ref, b_ref, c_ref, r_ref):
    kinds = ((False, False), (True, False), (False, True))
    r_ref[...] = rank_sum(at_ref, d_ref, (a_ref, b_ref, c_ref), kinds, None)


def rank_late_kernel(at_ref, d_ref, x_ref, early_ref, own_ref, send_ref, rest_ref):
    devices, rank, _ = send_ref.shape
    rows = early_ref.shape[1]
    total = rank_sum(at_ref, d_ref, (x_ref,), ((True, True),), early_ref[...])
    total = total.astype(BF16).astype(F32) * own_ref[...]
    rest_ref[...] = total[rank:].astype(BF16)
    first = total[:rank].astype(BF16)
    if rows < send_ref.shape[2]:
        send_ref[...] = jnp.zeros_like(send_ref)
    for d in range(devices):
        send_ref[d, :, :rows] = first


def split_kernel(at_ref, q_ref, l_ref, o_ref, dep_ref, heads_ref, half_ref):
    rank, _ = q_ref.shape
    devices, _, cols = heads_ref.shape
    for d in range(devices):
        heads_ref[d, :rank, :] = q_ref[:, d * cols : (d + 1) * cols]
        heads_ref[d, rank:, :] = l_ref[:, d * cols : (d + 1) * cols]
    width = half_ref.shape[2]
    for c in range(half_ref.shape[0]):
        start = pl.multiple_of((2 * c + 1 - at_ref[1]) * width, width)
        half_ref[c] = o_ref[:, pl.ds(start, width)]


def kv_kernel(x_ref, w_ref, own_ref, kup_ref, vup_ref, o_ref):
    devices, steps, _ = o_ref.shape
    rank, half = kup_ref.shape
    own = own_ref[...]
    both = nn(x_ref[...], w_ref[...])
    keys = both[:, :half] + SCALE * tn(own[:rank], kup_ref[...])
    values = both[:, half:] + SCALE * tn(own[rank:], vup_ref[...])
    for r in range(devices):
        for t in range(steps):
            m = t * devices + r
            o_ref[r, t : t + 1, :half] = keys[m : m + 1]
            o_ref[r, t : t + 1, half:] = values[m : m + 1]


def finish_kernel(q_ref, ranks_ref, mask_ref, up_ref, dep_ref, o_ref):
    devices, steps, _ = o_ref.shape
    rank = ranks_ref.shape[1]
    rows, _ = q_ref.shape
    u = ranks_ref[0].astype(F32)
    for d in range(1, devices):
        u = u + ranks_ref[d].astype(F32)
    u = u[:, :rows]
    spread = (jnp.concatenate([u] * devices, axis=0) * mask_ref[...]).astype(BF16)
    up = jnp.concatenate([up_ref[d, :rank] for d in range(devices)], axis=0)
    query = q_ref[...] + SCALE * tn(spread, up)
    for r in range(devices):
        for t in range(steps):
            m = t * devices + r
            o_ref[r, t : t + 1, :] = query[m : m + 1]


def rope(v, cosine, sine):
    return v * cosine + pltpu.roll(v, HEAD_WIDTH // 2, 1) * sine


def attend_kernel(len_ref, recv_ref, kv_ref, cos_ref, sin_ref, k_ref, v_ref, ctx_ref, ent_ref, q_s, kn_s, vn_s):
    devices, steps, cols = ctx_ref.shape
    slots, kv_cols = k_ref.shape
    kv_heads = kv_cols // HEAD_WIDTH
    per_device = cols // HEAD_WIDTH
    group = devices * per_device // kv_heads
    rows = group * steps
    score_scale = 1.0 / math.sqrt(HEAD_WIDTH)
    length = len_ref[0]
    kv = kv_ref[0]
    for d in range(1, devices):
        kv = kv + kv_ref[d]
    cosine = cos_ref[...]
    sine = sin_ref[...]
    kn_s[...] = jnp.zeros_like(kn_s)
    vn_s[...] = jnp.zeros_like(vn_s)
    fresh = kn_s.shape[0]
    col_old = lax.broadcasted_iota(jnp.int32, (rows, slots), 1)
    col_new = lax.broadcasted_iota(jnp.int32, (rows, fresh), 1)
    step_new = lax.rem(lax.broadcasted_iota(jnp.int32, (rows, fresh), 0), steps)
    for k in range(kv_heads):
        lanes = slice(k * HEAD_WIDTH, (k + 1) * HEAD_WIDTH)
        for i in range(group):
            h = k * group + i
            d, hh = h // per_device, h % per_device
            q_s[i * steps : (i + 1) * steps, :] = recv_ref[d, :, hh * HEAD_WIDTH : (hh + 1) * HEAD_WIDTH]
        query = q_s[...].astype(BF16).astype(F32)
        query = rope(query, cosine, sine).astype(BF16)
        key_now = rope(kv[:, lanes], cosine[:steps], sine[:steps]).astype(BF16).astype(F32)
        value_now = kv[:, kv_cols + k * HEAD_WIDTH : kv_cols + (k + 1) * HEAD_WIDTH].astype(BF16).astype(F32)
        ent_ref[:, lanes] = key_now
        ent_ref[:, kv_cols + k * HEAD_WIDTH : kv_cols + (k + 1) * HEAD_WIDTH] = value_now
        kn_s[:steps, :] = key_now
        vn_s[:steps, :] = value_now
        old = nt(query, k_ref[:, lanes]) * score_scale
        old = jnp.where(col_old < length, old, MASKED)
        new = nt(query, kn_s[...].astype(BF16)) * score_scale
        new = jnp.where((col_new < steps) & (col_new <= step_new), new, MASKED)
        top = jnp.maximum(jnp.max(old, axis=1, keepdims=True), jnp.max(new, axis=1, keepdims=True))
        e_old = jnp.exp(old - top)
        e_new = jnp.exp(new - top)
        total = jnp.sum(e_old, axis=1, keepdims=True) + jnp.sum(e_new, axis=1, keepdims=True)
        p_old = (e_old / total).astype(BF16)
        p_new = (e_new / total).astype(BF16)
        out = nn(p_old, v_ref[:, lanes]) + nn(p_new, vn_s[...].astype(BF16))
        out = out.astype(BF16).astype(F32)
        for i in range(group):
            h = k * group + i
            d, hh = h // per_device, h % per_device
            ctx_ref[d, :, hh * HEAD_WIDTH : (hh + 1) * HEAD_WIDTH] = out[i * steps : (i + 1) * steps, :]


def lower_kernel(ctx_ref, mask_ref, low_ref, x_ref, send_ref, x_s):
    devices, steps, _ = ctx_ref.shape
    rank = send_ref.shape[1]
    for r in range(devices):
        for t in range(steps):
            x_s[t * devices + r : t * devices + r + 1, :] = ctx_ref[r, t : t + 1, :]
    x = x_s[...].astype(BF16)
    x_ref[...] = x
    rows = x.shape[0]
    low = jnp.concatenate([low_ref[d, rank:] for d in range(devices)], axis=0)
    every = nt(low, x) * mask_ref[...]
    part = every[:rank]
    for d in range(1, devices):
        part = part + every[d * rank : (d + 1) * rank]
    if rows < send_ref.shape[2]:
        send_ref[...] = jnp.zeros_like(send_ref)
    for d in range(devices):
        send_ref[d, :, :rows] = part


def out_there_kernel(at_ref, x_ref, w_ref, o_ref):
    width = o_ref.shape[2]
    x = x_ref[...]
    for c in range(o_ref.shape[0]):
        start = pl.multiple_of((2 * c + 1 - at_ref[1]) * width, width)
        o_ref[c] = nn(x, w_ref[:, pl.ds(start, width)])


def out_here_kernel(at_ref, x_ref, w_ref, o_ref, w_s, sems):
    chips, _, width = o_ref.shape
    copies = []
    for c in range(chips):
        start = pl.multiple_of((2 * c + at_ref[1]) * width, width)
        copy = pltpu.make_async_copy(w_ref.at[:, pl.ds(start, width)], w_s.at[c], sems.at[c])
        copy.start()
        copies.append(copy)
    x = x_ref[...]
    for c in range(chips):
        copies[c].wait()
        o_ref[c] = nn(x, w_s[c])


def pair_kernel(at_ref, a_ref, b_ref, mask_ref, up_ref, other_ref, parts_ref, *outs):
    chips = len(outs)
    rows, width = outs[0].shape
    u = parts_ref[0]
    for d in range(1, parts_ref.shape[0]):
        u = u + parts_ref[d]
    u = u[:, :rows].astype(BF16).astype(F32)
    spread = jnp.concatenate([u * mask_ref[0:1, :], u * mask_ref[1:2, :]], axis=0).astype(BF16)
    for k, out in enumerate(outs):
        dest = lax.rem(at_ref[0] + k, chips)
        start = pl.multiple_of((2 * dest + at_ref[1]) * width, width)
        up = jnp.concatenate([up_ref[:, pl.ds(start, width)], other_ref[dest]], axis=0)
        out[...] = (a_ref[dest] + b_ref[dest] + SCALE * tn(spread, up)).astype(BF16)


def total_kernel(*refs):
    total = refs[0][...].astype(F32)
    for r in refs[1:-1]:
        total = total + r[...].astype(F32)
    refs[-1][...] = total.astype(BF16)


def body(
    tokens,
    query_weight,
    key_value_weight,
    output_weight,
    cached_rotated_keys,
    cached_values,
    lengths,
    request_adapter,
    adapter_pool_slot,
    adapter_down_maps,
    query_up_maps,
    key_up_maps,
    value_up_maps,
    result_lowering_factors,
    output_up_maps,
):
    both = ("tp", "sub")
    chips = lax.axis_size("tp")
    devices = lax.axis_size(both)
    lines = chips // 2
    me = lax.axis_index(both)
    core = lax.axis_index("sub")
    steps, requests, width = tokens.shape
    rows = steps * requests
    padded = -(-rows // 128) * 128
    cols = query_weight.shape[1]
    rank = key_up_maps.shape[1]
    assert devices == 2 * chips and chips % 2 == 0
    assert adapter_down_maps.shape[0] == 1 and requests == devices and cached_values.shape[0] == 1
    at = jnp.stack([lax.axis_index("tp"), core]).astype(jnp.int32)

    def swap_core(v):
        return lax.ppermute(v, "sub", [(0, 1), (1, 0)])

    def swap_y(v):
        return lax.ppermute(v, "tp", [(i, i ^ 1) for i in range(chips)])

    def shift_chip(v, k):
        if k == 0:
            return v
        return lax.ppermute(v, "tp", [(i, (i + k) % chips) for i in range(chips)])

    def exchange(v):
        return lax.all_to_all(v, both, 0, 0, tiled=True)

    x = tokens.reshape(rows, width)
    pieces = [shift_chip(x, 2 * k) for k in range(lines)]
    line = pl.pallas_call(
        stack_kernel,
        out_shape=jax.ShapeDtypeStruct((lines, rows, width), BF16),
        compiler_params=PARAMS,
    )(*pieces)
    across = swap_y(line)
    line_cross = swap_core(line)
    across_cross = swap_core(across)

    index = jnp.arange(devices, dtype=jnp.int32)
    slot = jnp.sum(
        jnp.where(request_adapter[:, None] == index[None, :], adapter_pool_slot[None, :], 0), axis=1
    )
    row_slot = jnp.tile(slot, steps)[None, :]
    spread_mask = (jnp.repeat(index, rank)[:, None] == row_slot).astype(F32)
    own_mask = (row_slot == me).astype(F32)
    pair_mask = (jnp.stack([me, me + 1 - 2 * core])[:, None] == row_slot).astype(F32)

    by_heads, half = pl.pallas_call(
        split_kernel,
        out_shape=(
            jax.ShapeDtypeStruct((devices, 2 * rank, cols), BF16),
            jax.ShapeDtypeStruct((chips, rank, width), BF16),
        ),
        in_specs=[SMEM, VMEM, VMEM, VMEM, ANY],
        compiler_params=PARAMS,
    )(at, query_up_maps[0], result_lowering_factors[0], output_up_maps[0], line)
    maps = exchange(by_heads)
    up_other = swap_core(half)

    query = query_stack(at, query_weight, line, False, False)
    query = query_stack(at, query_weight, line_cross, False, True, query)
    query = query_stack(at, query_weight, across, True, False, query)
    down = adapter_down_maps[0]
    early = pl.pallas_call(
        rank_early_kernel,
        out_shape=jax.ShapeDtypeStruct((down.shape[0], rows), F32),
        in_specs=[SMEM] + [VMEM] * 4,
        compiler_params=PARAMS,
    )(at, down, line, across, line_cross)
    rank_send, rank_rest = pl.pallas_call(
        rank_late_kernel,
        out_shape=(
            jax.ShapeDtypeStruct((devices, rank, padded), BF16),
            jax.ShapeDtypeStruct((2 * rank, rows), BF16),
        ),
        in_specs=[SMEM] + [VMEM] * 4,
        compiler_params=PARAMS,
    )(at, down, across_cross, early, own_mask)
    ranks = exchange(rank_send)
    kv_send = pl.pallas_call(
        kv_kernel,
        out_shape=jax.ShapeDtypeStruct((devices, steps, key_value_weight.shape[1]), F32),
        compiler_params=PARAMS,
    )(x, key_value_weight, rank_rest, key_up_maps[0], value_up_maps[0])
    kv = exchange(kv_send)
    query = query_stack(at, query_weight, across_cross, True, True, query)
    arrived = exchange(
        pl.pallas_call(
            finish_kernel,
            out_shape=jax.ShapeDtypeStruct((devices, steps, cols), F32),
            in_specs=[VMEM] * 4 + [ANY],
            compiler_params=PARAMS,
        )(query, ranks, spread_mask, maps, kv_send)
    )

    kv_cols = key_value_weight.shape[1] // 2
    half_width = HEAD_WIDTH // 2
    frequency = ROPE_BASE ** (-2.0 * jnp.arange(half_width, dtype=F32) / HEAD_WIDTH)
    positions = lengths[0] + jnp.arange(steps, dtype=jnp.int32)
    angles = positions.astype(F32)[:, None] * frequency
    cosine, sine = jnp.cos(angles), jnp.sin(angles)
    group = devices * cols // kv_cols
    cosine = jnp.tile(jnp.concatenate([cosine, cosine], axis=1), (group, 1))
    sine = jnp.tile(jnp.concatenate([-sine, sine], axis=1), (group, 1))
    context, fresh = pl.pallas_call(
        attend_kernel,
        out_shape=(
            jax.ShapeDtypeStruct((devices, steps, cols), F32),
            jax.ShapeDtypeStruct((steps, 2 * kv_cols), F32),
        ),
        in_specs=[SMEM] + [VMEM] * 6,
        scratch_shapes=[
            pltpu.VMEM((group * steps, HEAD_WIDTH), F32),
            pltpu.VMEM((16, HEAD_WIDTH), F32),
            pltpu.VMEM((16, HEAD_WIDTH), F32),
        ],
        compiler_params=PARAMS,
    )(lengths, arrived, kv, cosine, sine, cached_rotated_keys[0], cached_values[0])
    entries = fresh.astype(BF16)[:, None, :]

    by_head = exchange(context)
    lhs, part_send = pl.pallas_call(
        lower_kernel,
        out_shape=(
            jax.ShapeDtypeStruct((rows, cols), BF16),
            jax.ShapeDtypeStruct((devices, rank, padded), F32),
        ),
        scratch_shapes=[pltpu.VMEM((rows, cols), F32)],
        compiler_params=PARAMS,
    )(by_head, spread_mask, maps)
    parts = exchange(part_send)
    out_shape = jax.ShapeDtypeStruct((chips, rows, width), F32)
    out_there = pl.pallas_call(
        out_there_kernel,
        out_shape=out_shape,
        in_specs=[SMEM, VMEM, VMEM],
        compiler_params=PARAMS,
    )(at, lhs, output_weight)
    received = swap_core(out_there)
    out_here = pl.pallas_call(
        out_here_kernel,
        out_shape=out_shape,
        in_specs=[SMEM, VMEM, HBM],
        scratch_shapes=[
            pltpu.VMEM((chips, cols, width), BF16),
            pltpu.SemaphoreType.DMA((chips,)),
        ],
        compiler_params=WIDE,
    )(at, lhs, output_weight)
    chip_totals = pl.pallas_call(
        pair_kernel,
        out_shape=[jax.ShapeDtypeStruct((rows, width), BF16)] * chips,
        in_specs=[SMEM] + [VMEM] * 6,
        compiler_params=PARAMS,
    )(at, out_here, received, pair_mask, output_up_maps[0], up_other, parts)
    final = [shift_chip(v, k) for k, v in enumerate(chip_totals)]
    attended = pl.pallas_call(
        total_kernel,
        out_shape=jax.ShapeDtypeStruct((rows, width), BF16),
        compiler_params=PARAMS,
    )(*final)
    return attended.reshape(steps, requests, width), entries


def solution(mesh):
    placed = (
        P(None, "groups", ("tp", "sub")),
        P(None, ("tp", "sub")),
        P(("tp", "sub"), None),
        P(("tp", "sub"), None),
        P(("groups", "tp", "sub"), None, None),
        P(("groups", "tp", "sub"), None, None),
        P(("groups", "tp", "sub")),
        P("groups"),
        P(),
        P(("tp", "sub"), None, None),
        P(("tp", "sub"), None, None),
        P(("tp", "sub"), None, None),
        P(("tp", "sub"), None, None),
        P(("tp", "sub"), None, None),
        P(("tp", "sub"), None, None),
    )
    return jax.shard_map(
        body,
        mesh=mesh,
        in_specs=placed,
        out_specs=(P(None, "groups", ("tp", "sub")), P(None, ("groups", "tp", "sub"), None)),
        check_vma=False,
    )
```

```python
import functools
import math

import jax
import jax.numpy as jnp
from jax import lax
from jax.experimental import pallas as pl
from jax.experimental.pallas import tpu as pltpu
from jax.sharding import PartitionSpec as P

HEAD_WIDTH = 128
ROPE_BASE = 500000.0
MASKED = -1e30
SCALE = 0.5
F32 = jnp.float32
BF16 = jnp.bfloat16

PARAMS = pltpu.CompilerParams(vmem_limit_bytes=16 * 1024 * 1024)


def nn(a, b):
    return lax.dot_general(a, b, (((1,), (0,)), ((), ())), preferred_element_type=F32)


def nt(a, b):
    return lax.dot_general(a, b, (((1,), (1,)), ((), ())), preferred_element_type=F32)


def tn(a, b):
    return lax.dot_general(a, b, (((0,), (0,)), ((), ())), preferred_element_type=F32)


WIDE = pltpu.CompilerParams(vmem_limit_bytes=52 * 1024 * 1024)
VMEM = pl.BlockSpec(memory_space=pltpu.VMEM)
SMEM = pl.BlockSpec(memory_space=pltpu.SMEM)
ANY = pl.BlockSpec(memory_space=pl.ANY)
KINDS = ((False, False), (True, False), (False, True), (True, True))


def piece_at(at_ref, chips, k, flip, cross):
    lines = chips // 2
    z = lax.rem(at_ref[0] // 2 + lines - k, lines)
    y = lax.rem(at_ref[0], 2)
    core = 1 - at_ref[1] if cross else at_ref[1]
    return 4 * z + 2 * (1 - y if flip else y) + core


def stack_kernel(*refs):
    for k, r in enumerate(refs[:-1]):
        refs[-1][k] = r[...]


def stack(pieces):
    return pl.pallas_call(
        stack_kernel,
        out_shape=jax.ShapeDtypeStruct((len(pieces),) + pieces[0].shape, pieces[0].dtype),
        compiler_params=PARAMS,
    )(*pieces)


def query_kernel(at_ref, w_ref, a_ref, b_ref, c_ref, d_ref, dep_ref, q_ref, w_s, sems):
    lines, _, width = a_ref.shape
    copies = []
    for flip, cross in KINDS:
        for k in range(lines):
            i = len(copies)
            start = pl.multiple_of(piece_at(at_ref, 2 * lines, k, flip, cross) * width, width)
            copy = pltpu.make_async_copy(w_ref.at[pl.ds(start, width)], w_s.at[i], sems.at[i])
            copy.start()
            copies.append(copy)
    total = None
    for i, copy in enumerate(copies):
        x_ref = (a_ref, b_ref, c_ref, d_ref)[i // lines]
        copy.wait()
        part = nn(x_ref[i % lines], w_s[i])
        total = part if total is None else total + part
    q_ref[...] = total


def rank_kernel(at_ref, d_ref, a_ref, b_ref, c_ref, e_ref, own_ref, dep_ref, send_ref, rest_ref):
    lines, rows, width = a_ref.shape
    devices, rank, _ = send_ref.shape
    total = None
    for x_ref, (flip, cross) in zip((a_ref, b_ref, c_ref, e_ref), KINDS):
        for k in range(lines):
            start = pl.multiple_of(piece_at(at_ref, 2 * lines, k, flip, cross) * width, width)
            part = nt(d_ref[:, pl.ds(start, width)], x_ref[k])
            total = part if total is None else total + part
    total = total.astype(BF16).astype(F32) * own_ref[...]
    rest_ref[...] = total[rank:].astype(BF16)
    first = total[:rank].astype(BF16)
    if rows < send_ref.shape[2]:
        send_ref[...] = jnp.zeros_like(send_ref)
    for d in range(devices):
        send_ref[d, :, :rows] = first


def split_kernel(q_ref, heads_ref):
    devices, _, cols = heads_ref.shape
    for d in range(devices):
        heads_ref[d] = q_ref[:, d * cols : (d + 1) * cols]


def kv_kernel(x_ref, w_ref, own_ref, kup_ref, vup_ref, o_ref):
    rank, half = kup_ref.shape
    own = own_ref[...]
    both = nn(x_ref[...], w_ref[...])
    o_ref[:, :half] = both[:, :half] + SCALE * tn(own[:rank], kup_ref[...])
    o_ref[:, half:] = both[:, half:] + SCALE * tn(own[rank:], vup_ref[...])


def finish_kernel(q_ref, kv_ref, ranks_ref, mask_ref, up_ref, o_ref):
    devices, steps, _ = o_ref.shape
    rows, cols = q_ref.shape
    u = ranks_ref[0].astype(F32)
    for d in range(1, devices):
        u = u + ranks_ref[d].astype(F32)
    u = u[:, :rows]
    spread = (jnp.concatenate([u] * devices, axis=0) * mask_ref[...]).astype(BF16)
    up = jnp.concatenate([up_ref[d] for d in range(devices)], axis=0)
    query = q_ref[...] + SCALE * tn(spread, up)
    for r in range(devices):
        for t in range(steps):
            m = t * devices + r
            o_ref[r, t : t + 1, :cols] = query[m : m + 1]
            o_ref[r, t : t + 1, cols:] = kv_ref[m : m + 1, :]


def rope(v, cosine, sine):
    return v * cosine + pltpu.roll(v, HEAD_WIDTH // 2, 1) * sine


def attend_kernel(len_ref, recv_ref, cos_ref, sin_ref, k_ref, v_ref, dep_ref, ctx_ref, ent_ref, q_s, kn_s, vn_s):
    devices, steps, cols = recv_ref.shape
    cols -= 2 * k_ref.shape[1]
    slots, kv_cols = k_ref.shape
    kv_heads = kv_cols // HEAD_WIDTH
    per_device = cols // HEAD_WIDTH
    group = devices * per_device // kv_heads
    rows = group * steps
    score_scale = 1.0 / math.sqrt(HEAD_WIDTH)
    length = len_ref[0]
    kv = recv_ref[0, :, cols:]
    for d in range(1, devices):
        kv = kv + recv_ref[d, :, cols:]
    cosine = cos_ref[...]
    sine = sin_ref[...]
    kn_s[...] = jnp.zeros_like(kn_s)
    vn_s[...] = jnp.zeros_like(vn_s)
    fresh = kn_s.shape[0]
    col_old = lax.broadcasted_iota(jnp.int32, (rows, slots), 1)
    col_new = lax.broadcasted_iota(jnp.int32, (rows, fresh), 1)
    step_new = lax.rem(lax.broadcasted_iota(jnp.int32, (rows, fresh), 0), steps)
    for k in range(kv_heads):
        lanes = slice(k * HEAD_WIDTH, (k + 1) * HEAD_WIDTH)
        for i in range(group):
            h = k * group + i
            d, hh = h // per_device, h % per_device
            q_s[i * steps : (i + 1) * steps, :] = recv_ref[d, :, hh * HEAD_WIDTH : (hh + 1) * HEAD_WIDTH]
        query = q_s[...].astype(BF16).astype(F32)
        query = rope(query, cosine, sine).astype(BF16)
        key_now = rope(kv[:, lanes], cosine[:steps], sine[:steps]).astype(BF16).astype(F32)
        value_now = kv[:, kv_cols + k * HEAD_WIDTH : kv_cols + (k + 1) * HEAD_WIDTH].astype(BF16).astype(F32)
        ent_ref[:, lanes] = key_now
        ent_ref[:, kv_cols + k * HEAD_WIDTH : kv_cols + (k + 1) * HEAD_WIDTH] = value_now
        kn_s[:steps, :] = key_now
        vn_s[:steps, :] = value_now
        old = nt(query, k_ref[:, lanes]) * score_scale
        old = jnp.where(col_old < length, old, MASKED)
        new = nt(query, kn_s[...].astype(BF16)) * score_scale
        new = jnp.where((col_new < steps) & (col_new <= step_new), new, MASKED)
        top = jnp.maximum(jnp.max(old, axis=1, keepdims=True), jnp.max(new, axis=1, keepdims=True))
        e_old = jnp.exp(old - top)
        e_new = jnp.exp(new - top)
        total = jnp.sum(e_old, axis=1, keepdims=True) + jnp.sum(e_new, axis=1, keepdims=True)
        p_old = (e_old / total).astype(BF16)
        p_new = (e_new / total).astype(BF16)
        out = nn(p_old, v_ref[:, lanes]) + nn(p_new, vn_s[...].astype(BF16))
        ctx_ref[k * rows : (k + 1) * rows, :] = out.astype(BF16)


def lower_kernel(at_ref, low_ref, own_ref, a_ref, b_ref, c_ref, d_ref, x_ref, rank_ref, c_s, x_s):
    lines, per_row, head = a_ref.shape
    devices = 4 * lines
    rows, cols = x_ref.shape
    steps = rows // devices
    for r, (flip, cross) in zip((a_ref, b_ref, c_ref, d_ref), KINDS):
        for k in range(lines):
            start = pl.multiple_of(piece_at(at_ref, 2 * lines, k, flip, cross) * per_row, per_row)
            c_s[pl.ds(start, per_row), :] = r[k].astype(F32)
    for h in range(per_row // steps):
        for t in range(steps):
            piece = c_s[pl.ds(h * steps + t, devices, stride=per_row), :]
            x_s[t * devices : (t + 1) * devices, h * head : (h + 1) * head] = piece.astype(BF16)
    rank_ref[...] = (nt(low_ref[...], x_s[...]).astype(BF16).astype(F32) * own_ref[...]).astype(BF16)
    start = pl.multiple_of((2 * at_ref[0] + at_ref[1]) * cols, cols)
    x_ref[...] = x_s[:, pl.ds(start, cols)]


def fetch_kernel(at_ref, w_ref, dep_ref, there_ref, here_ref, sems):
    chips, _, width = there_ref.shape
    copies = []
    for half, (core, out_ref) in enumerate(((1 - at_ref[1], there_ref), (at_ref[1], here_ref))):
        for c in range(chips):
            start = pl.multiple_of((2 * c + core) * width, width)
            copy = pltpu.make_async_copy(
                w_ref.at[:, pl.ds(start, width)], out_ref.at[c], sems.at[half * chips + c]
            )
            copy.start()
            copies.append(copy)
    for copy in copies:
        copy.wait()


def out_kernel(cross, at_ref, x_ref, w_ref, rank_ref, up_ref, o_ref):
    width = o_ref.shape[2]
    core = 1 - at_ref[1] if cross else at_ref[1]
    x = x_ref[...]
    rank = rank_ref[...]
    for c in range(o_ref.shape[0]):
        lanes = pl.ds(pl.multiple_of((2 * c + core) * width, width), width)
        o_ref[c] = nn(x, w_ref[c]) + SCALE * tn(rank, up_ref[:, lanes])


def pair_kernel(at_ref, a_ref, b_ref, *outs):
    chips = len(outs)
    for k, out in enumerate(outs):
        dest = lax.rem(at_ref[0] + k, chips)
        out[...] = (a_ref[dest] + b_ref[dest]).astype(BF16)


def total_kernel(*refs):
    total = refs[0][...].astype(F32)
    for r in refs[1:-1]:
        total = total + r[...].astype(F32)
    refs[-1][...] = total.astype(BF16)


def body(
    tokens,
    query_weight,
    key_value_weight,
    output_weight,
    cached_rotated_keys,
    cached_values,
    lengths,
    request_adapter,
    adapter_pool_slot,
    adapter_down_maps,
    query_up_maps,
    key_up_maps,
    value_up_maps,
    result_lowering_factors,
    output_up_maps,
):
    both = ("tp", "sub")
    chips = lax.axis_size("tp")
    devices = lax.axis_size(both)
    lines = chips // 2
    me = lax.axis_index(both)
    steps, requests, width = tokens.shape
    rows = steps * requests
    padded = -(-rows // 128) * 128
    cols = query_weight.shape[1]
    rank = key_up_maps.shape[1]
    assert devices == 2 * chips and chips % 2 == 0
    assert adapter_down_maps.shape[0] == 1 and requests == devices and cached_values.shape[0] == 1
    at = jnp.stack([lax.axis_index("tp"), lax.axis_index("sub")]).astype(jnp.int32)

    def swap_core(v):
        return lax.ppermute(v, "sub", [(0, 1), (1, 0)])

    def swap_y(v):
        return lax.ppermute(v, "tp", [(i, i ^ 1) for i in range(chips)])

    def shift_chip(v, k):
        if k == 0:
            return v
        return lax.ppermute(v, "tp", [(i, (i + k) % chips) for i in range(chips)])

    def exchange(v):
        return lax.all_to_all(v, both, 0, 0, tiled=True)

    def gather(v):
        line = stack([shift_chip(v, 2 * k) for k in range(lines)])
        across = swap_y(line)
        return line, across, swap_core(line), swap_core(across)

    x = tokens.reshape(rows, width)
    down = adapter_down_maps[0]
    gathered = gather(x)

    index = jnp.arange(devices, dtype=jnp.int32)
    slot = jnp.sum(
        jnp.where(request_adapter[:, None] == index[None, :], adapter_pool_slot[None, :], 0), axis=1
    )
    row_slot = jnp.tile(slot, steps)[None, :]
    spread_mask = (jnp.repeat(index, rank)[:, None] == row_slot).astype(F32)
    own_mask = (row_slot == me).astype(F32)

    ups = exchange(
        pl.pallas_call(
            split_kernel,
            out_shape=jax.ShapeDtypeStruct((devices, rank, cols), BF16),
            compiler_params=PARAMS,
        )(query_up_maps[0])
    )
    rank_send, rank_rest = pl.pallas_call(
        rank_kernel,
        out_shape=(
            jax.ShapeDtypeStruct((devices, rank, padded), BF16),
            jax.ShapeDtypeStruct((2 * rank, rows), BF16),
        ),
        in_specs=[SMEM] + [VMEM] * 6 + [ANY],
        compiler_params=PARAMS,
    )(at, down, *gathered, own_mask, ups)
    ranks = exchange(rank_send)
    query = pl.pallas_call(
        query_kernel,
        out_shape=jax.ShapeDtypeStruct((rows, cols), F32),
        in_specs=[SMEM, ANY] + [VMEM] * 4 + [ANY],
        scratch_shapes=[
            pltpu.VMEM((devices, width, cols), BF16),
            pltpu.SemaphoreType.DMA((devices,)),
        ],
        compiler_params=WIDE,
    )(at, query_weight, *gathered, rank_send)
    kv_width = key_value_weight.shape[1]
    kv = pl.pallas_call(
        kv_kernel,
        out_shape=jax.ShapeDtypeStruct((rows, kv_width), F32),
        compiler_params=PARAMS,
    )(x, key_value_weight, rank_rest, key_up_maps[0], value_up_maps[0])
    to_rows = pl.pallas_call(
        finish_kernel,
        out_shape=jax.ShapeDtypeStruct((devices, steps, cols + kv_width), F32),
        compiler_params=PARAMS,
    )(query, kv, ranks, spread_mask, ups)
    arrived = exchange(to_rows)
    fetched = pl.pallas_call(
        fetch_kernel,
        out_shape=[jax.ShapeDtypeStruct((chips, cols, width), BF16)] * 2,
        in_specs=[SMEM, ANY, ANY],
        out_specs=[ANY, ANY],
        scratch_shapes=[pltpu.SemaphoreType.DMA((devices,))],
        compiler_params=pltpu.CompilerParams(vmem_limit_bytes=36 * 1024 * 1024),
    )(at, output_weight, to_rows)

    half_width = HEAD_WIDTH // 2
    frequency = ROPE_BASE ** (-2.0 * jnp.arange(half_width, dtype=F32) / HEAD_WIDTH)
    positions = lengths[0] + jnp.arange(steps, dtype=jnp.int32)
    angles = positions.astype(F32)[:, None] * frequency
    cosine, sine = jnp.cos(angles), jnp.sin(angles)
    group = 2 * devices * cols // kv_width
    heads = devices * cols // HEAD_WIDTH
    cosine = jnp.tile(jnp.concatenate([cosine, cosine], axis=1), (group, 1))
    sine = jnp.tile(jnp.concatenate([-sine, sine], axis=1), (group, 1))
    context, fresh = pl.pallas_call(
        attend_kernel,
        out_shape=(
            jax.ShapeDtypeStruct((heads * steps, HEAD_WIDTH), BF16),
            jax.ShapeDtypeStruct((steps, kv_width), F32),
        ),
        in_specs=[SMEM] + [VMEM] * 5 + [ANY],
        scratch_shapes=[
            pltpu.VMEM((group * steps, HEAD_WIDTH), F32),
            pltpu.VMEM((16, HEAD_WIDTH), F32),
            pltpu.VMEM((16, HEAD_WIDTH), F32),
        ],
        compiler_params=PARAMS,
    )(lengths, arrived, cosine, sine, cached_rotated_keys[0], cached_values[0], fetched[0])
    entries = fresh.astype(BF16)[:, None, :]

    lhs, out_rank = pl.pallas_call(
        lower_kernel,
        out_shape=(
            jax.ShapeDtypeStruct((rows, cols), BF16),
            jax.ShapeDtypeStruct((rank, rows), BF16),
        ),
        in_specs=[SMEM] + [VMEM] * 6,
        scratch_shapes=[
            pltpu.VMEM((devices * heads * steps, HEAD_WIDTH), F32),
            pltpu.VMEM((rows, heads * HEAD_WIDTH), BF16),
        ],
        compiler_params=PARAMS,
    )(at, result_lowering_factors[0], own_mask, *gather(context))

    def out_half(cross):
        return pl.pallas_call(
            functools.partial(out_kernel, cross),
            out_shape=jax.ShapeDtypeStruct((chips, rows, width), F32),
            in_specs=[SMEM] + [VMEM] * 4,
            compiler_params=PARAMS,
        )(at, lhs, fetched[0 if cross else 1], out_rank, output_up_maps[0])

    received = swap_core(out_half(True))
    chip_totals = pl.pallas_call(
        pair_kernel,
        out_shape=[jax.ShapeDtypeStruct((rows, width), BF16)] * chips,
        in_specs=[SMEM, VMEM, VMEM],
        compiler_params=PARAMS,
    )(at, out_half(False), received)
    final = [shift_chip(v, k) for k, v in enumerate(chip_totals)]
    attended = pl.pallas_call(
        total_kernel,
        out_shape=jax.ShapeDtypeStruct((rows, width), BF16),
        compiler_params=PARAMS,
    )(*final)
    return attended.reshape(steps, requests, width), entries


def solution(mesh):
    placed = (
        P(None, "groups", ("tp", "sub")),
        P(None, ("tp", "sub")),
        P(("tp", "sub"), None),
        P(("tp", "sub"), None),
        P(("groups", "tp", "sub"), None, None),
        P(("groups", "tp", "sub"), None, None),
        P(("groups", "tp", "sub")),
        P("groups"),
        P(),
        P(("tp", "sub"), None, None),
        P(("tp", "sub"), None, None),
        P(("tp", "sub"), None, None),
        P(("tp", "sub"), None, None),
        P(("tp", "sub"), None, None),
        P(("tp", "sub"), None, None),
    )
    return jax.shard_map(
        body,
        mesh=mesh,
        in_specs=placed,
        out_specs=(P(None, "groups", ("tp", "sub")), P(None, ("groups", "tp", "sub"), None)),
        check_vma=False,
    )
```

```python
import functools
import math

import jax
import jax.numpy as jnp
from jax import lax
from jax.experimental import pallas as pl
from jax.experimental.pallas import tpu as pltpu
from jax.sharding import PartitionSpec as P

HEAD_WIDTH = 128
ROPE_BASE = 500000.0
MASKED = -1e30
SCALE = 0.5
F32 = jnp.float32
BF16 = jnp.bfloat16

PARAMS = pltpu.CompilerParams(vmem_limit_bytes=16 * 1024 * 1024)


def nn(a, b):
    return lax.dot_general(a, b, (((1,), (0,)), ((), ())), preferred_element_type=F32)


def nt(a, b):
    return lax.dot_general(a, b, (((1,), (1,)), ((), ())), preferred_element_type=F32)


def tn(a, b):
    return lax.dot_general(a, b, (((0,), (0,)), ((), ())), preferred_element_type=F32)


WIDE = pltpu.CompilerParams(vmem_limit_bytes=24 * 1024 * 1024)
VMEM = pl.BlockSpec(memory_space=pltpu.VMEM)
SMEM = pl.BlockSpec(memory_space=pltpu.SMEM)
ANY = pl.BlockSpec(memory_space=pl.ANY)
KINDS = ((False, False), (True, False), (False, True), (True, True))


def piece_at(at_ref, chips, k, flip, cross):
    lines = chips // 2
    z = lax.rem(at_ref[0] // 2 + lines - k, lines)
    y = lax.rem(at_ref[0], 2)
    core = 1 - at_ref[1] if cross else at_ref[1]
    return 4 * z + 2 * (1 - y if flip else y) + core


def stack_kernel(*refs):
    for k, r in enumerate(refs[:-1]):
        refs[-1][k] = r[...]


def stack(pieces):
    return pl.pallas_call(
        stack_kernel,
        out_shape=jax.ShapeDtypeStruct((len(pieces),) + pieces[0].shape, pieces[0].dtype),
        compiler_params=PARAMS,
    )(*pieces)


def query_kernel(at_ref, w_ref, a_ref, b_ref, c_ref, d_ref, dep_ref, q_ref, w_s, sems):
    lines, _, width = a_ref.shape
    copies = []
    for flip, cross in KINDS:
        for k in range(lines):
            i = len(copies)
            start = pl.multiple_of(piece_at(at_ref, 2 * lines, k, flip, cross) * width, width)
            copy = pltpu.make_async_copy(w_ref.at[pl.ds(start, width)], w_s.at[i], sems.at[i])
            copy.start()
            copies.append(copy)
    total = None
    for i, copy in enumerate(copies):
        x_ref = (a_ref, b_ref, c_ref, d_ref)[i // lines]
        copy.wait()
        part = nn(x_ref[i % lines], w_s[i])
        total = part if total is None else total + part
    q_ref[...] = total


def rank_kernel(at_ref, d_ref, a_ref, b_ref, c_ref, e_ref, own_ref, send_ref, rest_ref):
    lines, rows, width = a_ref.shape
    devices, rank, _ = send_ref.shape
    total = None
    for x_ref, (flip, cross) in zip((a_ref, b_ref, c_ref, e_ref), KINDS):
        for k in range(lines):
            start = pl.multiple_of(piece_at(at_ref, 2 * lines, k, flip, cross) * width, width)
            part = nt(d_ref[:, pl.ds(start, width)], x_ref[k])
            total = part if total is None else total + part
    total = total.astype(BF16).astype(F32) * own_ref[...]
    rest_ref[...] = total[rank:].astype(BF16)
    first = total[:rank].astype(BF16)
    if rows < send_ref.shape[2]:
        send_ref[...] = jnp.zeros_like(send_ref)
    for d in range(devices):
        send_ref[d, :, :rows] = first


def run_copies(pairs, sems):
    copies = [pltpu.make_async_copy(a, b, sems.at[i]) for i, (a, b) in enumerate(pairs)]
    for copy in copies:
        copy.start()
    for copy in copies:
        copy.wait()


def split_kernel(m_ref, x_ref, heads_ref, out_ref, sems):
    devices, _, cols = heads_ref.shape
    pieces = [(m_ref.at[:, d * cols : (d + 1) * cols], heads_ref.at[d]) for d in range(devices)]
    run_copies([(x_ref, out_ref)] + pieces, sems)


def ahead_kernel(dep_ref, *refs):
    count = (len(refs) - 1) // 2
    run_copies(list(zip(refs[:count], refs[count : 2 * count])), refs[-1])


def in_hbm(v):
    return pltpu.with_memory_space_constraint(v, pltpu.HBM)


def ahead(dep, *arrays):
    return pl.pallas_call(
        ahead_kernel,
        out_shape=[jax.ShapeDtypeStruct(v.shape, v.dtype) for v in arrays],
        in_specs=[ANY] * (1 + len(arrays)),
        out_specs=[ANY] * len(arrays),
        scratch_shapes=[pltpu.SemaphoreType.DMA((len(arrays),))],
        compiler_params=PARAMS,
    )(dep, *[in_hbm(v) for v in arrays])


def pass_kernel(x_ref, dep_ref, o_ref):
    o_ref[...] = x_ref[...]


def kv_kernel(x_ref, w_ref, own_ref, kup_ref, vup_ref, o_ref):
    rank, half = kup_ref.shape
    own = own_ref[...]
    both = nn(x_ref[...], w_ref[...])
    o_ref[:, :half] = both[:, :half] + SCALE * tn(own[:rank], kup_ref[...])
    o_ref[:, half:] = both[:, half:] + SCALE * tn(own[rank:], vup_ref[...])


def finish_kernel(q_ref, kv_ref, ranks_ref, mask_ref, up_ref, o_ref):
    devices, steps, _ = o_ref.shape
    rows, cols = q_ref.shape
    u = ranks_ref[0].astype(F32)
    for d in range(1, devices):
        u = u + ranks_ref[d].astype(F32)
    u = u[:, :rows]
    spread = (jnp.concatenate([u] * devices, axis=0) * mask_ref[...]).astype(BF16)
    up = jnp.concatenate([up_ref[d] for d in range(devices)], axis=0)
    query = q_ref[...] + SCALE * tn(spread, up)
    for r in range(devices):
        for t in range(steps):
            m = t * devices + r
            o_ref[r, t : t + 1, :cols] = query[m : m + 1]
            o_ref[r, t : t + 1, cols:] = kv_ref[m : m + 1, :]


def rope(v, cosine, sine):
    return v * cosine + pltpu.roll(v, HEAD_WIDTH // 2, 1) * sine


def attend_kernel(len_ref, recv_ref, cos_ref, sin_ref, k_ref, v_ref, dep_ref, ctx_ref, ent_ref, q_s, kn_s, vn_s):
    devices, steps, cols = recv_ref.shape
    cols -= 2 * k_ref.shape[1]
    slots, kv_cols = k_ref.shape
    kv_heads = kv_cols // HEAD_WIDTH
    per_device = cols // HEAD_WIDTH
    group = devices * per_device // kv_heads
    rows = group * steps
    score_scale = 1.0 / math.sqrt(HEAD_WIDTH)
    length = len_ref[0]
    kv = recv_ref[0, :, cols:]
    for d in range(1, devices):
        kv = kv + recv_ref[d, :, cols:]
    cosine = cos_ref[...]
    sine = sin_ref[...]
    kn_s[...] = jnp.zeros_like(kn_s)
    vn_s[...] = jnp.zeros_like(vn_s)
    fresh = kn_s.shape[0]
    col_old = lax.broadcasted_iota(jnp.int32, (rows, slots), 1)
    col_new = lax.broadcasted_iota(jnp.int32, (rows, fresh), 1)
    step_new = lax.rem(lax.broadcasted_iota(jnp.int32, (rows, fresh), 0), steps)
    for k in range(kv_heads):
        lanes = slice(k * HEAD_WIDTH, (k + 1) * HEAD_WIDTH)
        for i in range(group):
            h = k * group + i
            d, hh = h // per_device, h % per_device
            q_s[i * steps : (i + 1) * steps, :] = recv_ref[d, :, hh * HEAD_WIDTH : (hh + 1) * HEAD_WIDTH]
        query = q_s[...].astype(BF16).astype(F32)
        query = rope(query, cosine, sine).astype(BF16)
        key_now = rope(kv[:, lanes], cosine[:steps], sine[:steps]).astype(BF16).astype(F32)
        value_now = kv[:, kv_cols + k * HEAD_WIDTH : kv_cols + (k + 1) * HEAD_WIDTH].astype(BF16).astype(F32)
        ent_ref[:, lanes] = key_now
        ent_ref[:, kv_cols + k * HEAD_WIDTH : kv_cols + (k + 1) * HEAD_WIDTH] = value_now
        kn_s[:steps, :] = key_now
        vn_s[:steps, :] = value_now
        old = nt(query, k_ref[:, lanes]) * score_scale
        old = jnp.where(col_old < length, old, MASKED)
        new = nt(query, kn_s[...].astype(BF16)) * score_scale
        new = jnp.where((col_new < steps) & (col_new <= step_new), new, MASKED)
        top = jnp.maximum(jnp.max(old, axis=1, keepdims=True), jnp.max(new, axis=1, keepdims=True))
        e_old = jnp.exp(old - top)
        e_new = jnp.exp(new - top)
        total = jnp.sum(e_old, axis=1, keepdims=True) + jnp.sum(e_new, axis=1, keepdims=True)
        p_old = (e_old / total).astype(BF16)
        p_new = (e_new / total).astype(BF16)
        out = nn(p_old, v_ref[:, lanes]) + nn(p_new, vn_s[...].astype(BF16))
        ctx_ref[k * rows : (k + 1) * rows, :] = out.astype(BF16)


def lower_kernel(at_ref, low_ref, own_ref, a_ref, b_ref, c_ref, d_ref, x_ref, rank_ref, c_s, x_s):
    lines, per_row, head = a_ref.shape
    devices = 4 * lines
    rows, cols = x_ref.shape
    steps = rows // devices
    for r, (flip, cross) in zip((a_ref, b_ref, c_ref, d_ref), KINDS):
        for k in range(lines):
            start = pl.multiple_of(piece_at(at_ref, 2 * lines, k, flip, cross) * per_row, per_row)
            c_s[pl.ds(start, per_row), :] = r[k].astype(F32)
    for h in range(per_row // steps):
        for t in range(steps):
            piece = c_s[pl.ds(h * steps + t, devices, stride=per_row), :]
            x_s[t * devices : (t + 1) * devices, h * head : (h + 1) * head] = piece.astype(BF16)
    rank_ref[...] = (nt(low_ref[...], x_s[...]).astype(BF16).astype(F32) * own_ref[...]).astype(BF16)
    start = pl.multiple_of((2 * at_ref[0] + at_ref[1]) * cols, cols)
    x_ref[...] = x_s[:, pl.ds(start, cols)]


def fetch_kernel(at_ref, w_ref, dep_ref, there_ref, here_ref, sems):
    chips, _, width = there_ref.shape
    copies = []
    for half, (core, out_ref) in enumerate(((1 - at_ref[1], there_ref), (at_ref[1], here_ref))):
        for c in range(chips):
            start = pl.multiple_of((2 * c + core) * width, width)
            copy = pltpu.make_async_copy(
                w_ref.at[:, pl.ds(start, width)], out_ref.at[c], sems.at[half * chips + c]
            )
            copy.start()
            copies.append(copy)
    for copy in copies:
        copy.wait()


def out_kernel(cross, places, at_ref, x_ref, w_ref, rank_ref, up_ref, o_ref):
    width = o_ref.shape[2]
    chips = w_ref.shape[0]
    core = 1 - at_ref[1] if cross else at_ref[1]
    x = x_ref[...]
    rank = rank_ref[...]
    for i, k in enumerate(places):
        dest = lax.rem(at_ref[0] + k, chips)
        lanes = pl.ds(pl.multiple_of((2 * dest + core) * width, width), width)
        o_ref[i] = nn(x, w_ref[dest]) + SCALE * tn(rank, up_ref[:, lanes])


def pair_kernel(a_ref, b_ref, *outs):
    for i, out in enumerate(outs):
        out[...] = (a_ref[i] + b_ref[i]).astype(BF16)


def total_kernel(*refs):
    total = refs[0][...].astype(F32)
    for r in refs[1:-1]:
        total = total + r[...].astype(F32)
    refs[-1][...] = total.astype(BF16)


def body(
    tokens,
    query_weight,
    key_value_weight,
    output_weight,
    cached_rotated_keys,
    cached_values,
    lengths,
    request_adapter,
    adapter_pool_slot,
    adapter_down_maps,
    query_up_maps,
    key_up_maps,
    value_up_maps,
    result_lowering_factors,
    output_up_maps,
):
    both = ("tp", "sub")
    chips = lax.axis_size("tp")
    devices = lax.axis_size(both)
    lines = chips // 2
    me = lax.axis_index(both)
    steps, requests, width = tokens.shape
    rows = steps * requests
    padded = -(-rows // 128) * 128
    cols = query_weight.shape[1]
    rank = key_up_maps.shape[1]
    assert devices == 2 * chips and chips % 2 == 0
    assert adapter_down_maps.shape[0] == 1 and requests == devices and cached_values.shape[0] == 1
    at = jnp.stack([lax.axis_index("tp"), lax.axis_index("sub")]).astype(jnp.int32)

    def swap_core(v):
        return lax.ppermute(v, "sub", [(0, 1), (1, 0)])

    def swap_y(v):
        return lax.ppermute(v, "tp", [(i, i ^ 1) for i in range(chips)])

    def shift_chip(v, k):
        if k == 0:
            return v
        return lax.ppermute(v, "tp", [(i, (i + k) % chips) for i in range(chips)])

    def exchange(v):
        return lax.all_to_all(v, both, 0, 0, tiled=True)

    def gather(v, own, after=None):
        line = stack([own] + [shift_chip(v, 2 * k) for k in range(1, lines)])
        across = swap_y(line)
        if after is not None:
            across = pl.pallas_call(
                pass_kernel,
                out_shape=jax.ShapeDtypeStruct(across.shape, across.dtype),
                in_specs=[VMEM, ANY],
                compiler_params=PARAMS,
            )(across, after)
        return line, across, swap_core(line), swap_core(across)

    x = tokens.reshape(rows, width)
    by_heads, own_x = pl.pallas_call(
        split_kernel,
        out_shape=(
            jax.ShapeDtypeStruct((devices, rank, cols), BF16),
            jax.ShapeDtypeStruct((rows, width), BF16),
        ),
        in_specs=[ANY, ANY],
        out_specs=(ANY, ANY),
        scratch_shapes=[pltpu.SemaphoreType.DMA((devices + 1,))],
        compiler_params=PARAMS,
    )(in_hbm(query_up_maps[0]), in_hbm(x))
    ups = exchange(by_heads)
    gathered = gather(x, own_x, ups)
    down, kv_weight, key_up, value_up, old_keys, old_values, lowering, out_up = ahead(
        gathered[0],
        adapter_down_maps[0],
        key_value_weight,
        key_up_maps[0],
        value_up_maps[0],
        cached_rotated_keys[0],
        cached_values[0],
        result_lowering_factors[0],
        output_up_maps[0],
    )

    index = jnp.arange(devices, dtype=jnp.int32)
    slot = jnp.sum(
        jnp.where(request_adapter[:, None] == index[None, :], adapter_pool_slot[None, :], 0), axis=1
    )
    row_slot = jnp.tile(slot, steps)[None, :]
    spread_mask = (jnp.repeat(index, rank)[:, None] == row_slot).astype(F32)
    own_mask = (row_slot == me).astype(F32)

    rank_send, rank_rest = pl.pallas_call(
        rank_kernel,
        out_shape=(
            jax.ShapeDtypeStruct((devices, rank, padded), BF16),
            jax.ShapeDtypeStruct((2 * rank, rows), BF16),
        ),
        in_specs=[SMEM] + [VMEM] * 6,
        compiler_params=PARAMS,
    )(at, down, *gathered, own_mask)
    ranks = exchange(rank_send)
    query = pl.pallas_call(
        query_kernel,
        out_shape=jax.ShapeDtypeStruct((rows, cols), F32),
        in_specs=[SMEM, ANY] + [VMEM] * 4 + [ANY],
        scratch_shapes=[
            pltpu.VMEM((devices, width, cols), BF16),
            pltpu.SemaphoreType.DMA((devices,)),
        ],
        compiler_params=WIDE,
    )(at, in_hbm(query_weight), *gathered, rank_send)
    kv_width = key_value_weight.shape[1]
    kv = pl.pallas_call(
        kv_kernel,
        out_shape=jax.ShapeDtypeStruct((rows, kv_width), F32),
        compiler_params=PARAMS,
    )(own_x, kv_weight, rank_rest, key_up, value_up)
    to_rows = pl.pallas_call(
        finish_kernel,
        out_shape=jax.ShapeDtypeStruct((devices, steps, cols + kv_width), F32),
        compiler_params=PARAMS,
    )(query, kv, ranks, spread_mask, ups)
    arrived = exchange(to_rows)
    fetched = pl.pallas_call(
        fetch_kernel,
        out_shape=[jax.ShapeDtypeStruct((chips, cols, width), BF16)] * 2,
        in_specs=[SMEM, ANY, ANY],
        out_specs=[ANY, ANY],
        scratch_shapes=[pltpu.SemaphoreType.DMA((devices,))],
        compiler_params=PARAMS,
    )(at, in_hbm(output_weight), to_rows)

    half_width = HEAD_WIDTH // 2
    frequency = ROPE_BASE ** (-2.0 * jnp.arange(half_width, dtype=F32) / HEAD_WIDTH)
    positions = lengths[0] + jnp.arange(steps, dtype=jnp.int32)
    angles = positions.astype(F32)[:, None] * frequency
    cosine, sine = jnp.cos(angles), jnp.sin(angles)
    group = 2 * devices * cols // kv_width
    heads = devices * cols // HEAD_WIDTH
    cosine = jnp.tile(jnp.concatenate([cosine, cosine], axis=1), (group, 1))
    sine = jnp.tile(jnp.concatenate([-sine, sine], axis=1), (group, 1))
    context, fresh = pl.pallas_call(
        attend_kernel,
        out_shape=(
            jax.ShapeDtypeStruct((heads * steps, HEAD_WIDTH), BF16),
            jax.ShapeDtypeStruct((steps, kv_width), F32),
        ),
        in_specs=[SMEM] + [VMEM] * 5 + [ANY],
        scratch_shapes=[
            pltpu.VMEM((group * steps, HEAD_WIDTH), F32),
            pltpu.VMEM((16, HEAD_WIDTH), F32),
            pltpu.VMEM((16, HEAD_WIDTH), F32),
        ],
        compiler_params=PARAMS,
    )(lengths, arrived, cosine, sine, old_keys, old_values, fetched[0])
    entries = fresh.astype(BF16)[:, None, :]

    lhs, out_rank = pl.pallas_call(
        lower_kernel,
        out_shape=(
            jax.ShapeDtypeStruct((rows, cols), BF16),
            jax.ShapeDtypeStruct((rank, rows), BF16),
        ),
        in_specs=[SMEM] + [VMEM] * 6,
        scratch_shapes=[
            pltpu.VMEM((devices * heads * steps, HEAD_WIDTH), F32),
            pltpu.VMEM((rows, heads * HEAD_WIDTH), BF16),
        ],
        compiler_params=PARAMS,
    )(at, lowering, own_mask, *gather(context, context))

    def out_half(cross, places):
        return pl.pallas_call(
            functools.partial(out_kernel, cross, places),
            out_shape=jax.ShapeDtypeStruct((len(places), rows, width), F32),
            in_specs=[SMEM] + [VMEM] * 4,
            compiler_params=PARAMS,
        )(at, lhs, fetched[0 if cross else 1], out_rank, out_up)

    final = []
    first = list(range(chips // 4, chips - chips // 4))
    for places in (first, [k for k in range(chips) if k not in first]):
        received = swap_core(out_half(True, places))
        totals = pl.pallas_call(
            pair_kernel,
            out_shape=[jax.ShapeDtypeStruct((rows, width), BF16)] * len(places),
            compiler_params=PARAMS,
        )(out_half(False, places), received)
        final += [shift_chip(v, k) for k, v in zip(places, totals)]
    attended = pl.pallas_call(
        total_kernel,
        out_shape=jax.ShapeDtypeStruct((rows, width), BF16),
        compiler_params=PARAMS,
    )(*final)
    return attended.reshape(steps, requests, width), entries


def solution(mesh):
    placed = (
        P(None, "groups", ("tp", "sub")),
        P(None, ("tp", "sub")),
        P(("tp", "sub"), None),
        P(("tp", "sub"), None),
        P(("groups", "tp", "sub"), None, None),
        P(("groups", "tp", "sub"), None, None),
        P(("groups", "tp", "sub")),
        P("groups"),
        P(),
        P(("tp", "sub"), None, None),
        P(("tp", "sub"), None, None),
        P(("tp", "sub"), None, None),
        P(("tp", "sub"), None, None),
        P(("tp", "sub"), None, None),
        P(("tp", "sub"), None, None),
    )
    return jax.shard_map(
        body,
        mesh=mesh,
        in_specs=placed,
        out_specs=(P(None, "groups", ("tp", "sub")), P(None, ("groups", "tp", "sub"), None)),
        check_vma=False,
    )
```

```python
import functools
import math

import jax
import jax.numpy as jnp
from jax import lax
from jax.experimental import pallas as pl
from jax.experimental.pallas import tpu as pltpu
from jax.sharding import PartitionSpec as P

HEAD_WIDTH = 128
ROPE_BASE = 500000.0
MASKED = -1e30
SCALE = 0.5
F32 = jnp.float32
BF16 = jnp.bfloat16

PARAMS = pltpu.CompilerParams(vmem_limit_bytes=16 * 1024 * 1024)


def nn(a, b):
    return lax.dot_general(a, b, (((1,), (0,)), ((), ())), preferred_element_type=F32)


def nt(a, b):
    return lax.dot_general(a, b, (((1,), (1,)), ((), ())), preferred_element_type=F32)


def tn(a, b):
    return lax.dot_general(a, b, (((0,), (0,)), ((), ())), preferred_element_type=F32)


WIDE = pltpu.CompilerParams(vmem_limit_bytes=24 * 1024 * 1024)
VMEM = pl.BlockSpec(memory_space=pltpu.VMEM)
SMEM = pl.BlockSpec(memory_space=pltpu.SMEM)
ANY = pl.BlockSpec(memory_space=pl.ANY)
KINDS = ((False, False), (True, False), (False, True), (True, True))


def piece_at(at_ref, chips, k, flip, cross):
    lines = chips // 2
    z = lax.rem(at_ref[0] // 2 + lines - k, lines)
    y = lax.rem(at_ref[0], 2)
    core = 1 - at_ref[1] if cross else at_ref[1]
    return 4 * z + 2 * (1 - y if flip else y) + core


def stack_kernel(count, *refs):
    for k in range(count):
        refs[-1][k] = refs[k][...]


def stack(pieces, *deps):
    return pl.pallas_call(
        functools.partial(stack_kernel, len(pieces)),
        out_shape=jax.ShapeDtypeStruct((len(pieces),) + pieces[0].shape, pieces[0].dtype),
        in_specs=[VMEM] * len(pieces) + [ANY] * len(deps),
        compiler_params=PARAMS,
    )(*pieces, *deps)


def query_kernel(at_ref, w_ref, kw_ref, kup_ref, vup_ref, own_ref, x_ref, a_ref, b_ref, c_ref, d_ref, *refs):
    dep_ref, q_ref, kv_ref, w_s, kw_s, kup_s, vup_s, sems, kv_sems = refs
    lines, _, width = a_ref.shape
    kv_copies = [
        pltpu.make_async_copy(source, target, kv_sems.at[i])
        for i, (source, target) in enumerate(((kw_ref, kw_s), (kup_ref, kup_s), (vup_ref, vup_s)))
    ]
    copies = []
    for flip, cross in KINDS:
        for k in range(lines):
            i = len(copies)
            start = pl.multiple_of(piece_at(at_ref, 2 * lines, k, flip, cross) * width, width)
            copies.append(pltpu.make_async_copy(w_ref.at[pl.ds(start, width)], w_s.at[i], sems.at[i]))
    for copy in kv_copies + copies:
        copy.start()
    for copy in kv_copies:
        copy.wait()
    rank, half = kup_s.shape
    own = own_ref[...]
    both = nn(x_ref[...], kw_s[...])
    kv_ref[:, :half] = both[:, :half] + SCALE * tn(own[:rank], kup_s[...])
    kv_ref[:, half:] = both[:, half:] + SCALE * tn(own[rank:], vup_s[...])
    total = None
    for i, copy in enumerate(copies):
        stack_ref = (a_ref, b_ref, c_ref, d_ref)[i // lines]
        copy.wait()
        part = nn(stack_ref[i % lines], w_s[i])
        total = part if total is None else total + part
    q_ref[...] = total


def rank_kernel(at_ref, d_ref, a_ref, b_ref, c_ref, e_ref, own_ref, send_ref, rest_ref):
    lines, rows, width = a_ref.shape
    devices, rank, _ = send_ref.shape
    total = None
    for x_ref, (flip, cross) in zip((a_ref, b_ref, c_ref, e_ref), KINDS):
        for k in range(lines):
            start = pl.multiple_of(piece_at(at_ref, 2 * lines, k, flip, cross) * width, width)
            part = nt(d_ref[:, pl.ds(start, width)], x_ref[k])
            total = part if total is None else total + part
    total = total.astype(BF16).astype(F32) * own_ref[...]
    rest_ref[...] = total[rank:].astype(BF16)
    first = total[:rank].astype(BF16)
    if rows < send_ref.shape[2]:
        send_ref[...] = jnp.zeros_like(send_ref)
    for d in range(devices):
        send_ref[d, :, :rows] = first


def run_copies(pairs, sems):
    copies = [pltpu.make_async_copy(a, b, sems.at[i]) for i, (a, b) in enumerate(pairs)]
    for copy in copies:
        copy.start()
    for copy in copies:
        copy.wait()


def split_kernel(m_ref, dep_ref, heads_ref):
    devices, _, cols = heads_ref.shape
    for d in range(devices):
        heads_ref[d] = m_ref[:, d * cols : (d + 1) * cols]


def ahead_kernel(dep_ref, *refs):
    count = (len(refs) - 1) // 2
    run_copies(list(zip(refs[:count], refs[count : 2 * count])), refs[-1])


def in_hbm(v):
    return pltpu.with_memory_space_constraint(v, pltpu.HBM)


def ahead(dep, *arrays):
    return pl.pallas_call(
        ahead_kernel,
        out_shape=[jax.ShapeDtypeStruct(v.shape, v.dtype) for v in arrays],
        in_specs=[ANY] * (1 + len(arrays)),
        out_specs=[ANY] * len(arrays),
        scratch_shapes=[pltpu.SemaphoreType.DMA((len(arrays),))],
        compiler_params=PARAMS,
    )(dep, *[in_hbm(v) for v in arrays])


def pass_kernel(x_ref, dep_ref, o_ref):
    o_ref[...] = x_ref[...]


def finish_kernel(q_ref, kv_ref, ranks_ref, mask_ref, up_ref, o_ref):
    devices, steps, _ = o_ref.shape
    rows, cols = q_ref.shape
    u = ranks_ref[0].astype(F32)
    for d in range(1, devices):
        u = u + ranks_ref[d].astype(F32)
    u = u[:, :rows]
    spread = (jnp.concatenate([u] * devices, axis=0) * mask_ref[...]).astype(BF16)
    up = jnp.concatenate([up_ref[d] for d in range(devices)], axis=0)
    query = q_ref[...] + SCALE * tn(spread, up)
    for r in range(devices):
        for t in range(steps):
            m = t * devices + r
            o_ref[r, t : t + 1, :cols] = query[m : m + 1]
            o_ref[r, t : t + 1, cols:] = kv_ref[m : m + 1, :]


def rope(v, cosine, sine):
    return v * cosine + pltpu.roll(v, HEAD_WIDTH // 2, 1) * sine


def attend_kernel(len_ref, recv_ref, cos_ref, sin_ref, k_hbm, v_hbm, ctx_ref, ent_ref, q_s, kn_s, vn_s, k_ref, v_ref, sems):
    copies = [
        pltpu.make_async_copy(k_hbm, k_ref, sems.at[0]),
        pltpu.make_async_copy(v_hbm, v_ref, sems.at[1]),
    ]
    for copy in copies:
        copy.start()
    devices, steps, cols = recv_ref.shape
    cols -= 2 * k_ref.shape[1]
    slots, kv_cols = k_ref.shape
    kv_heads = kv_cols // HEAD_WIDTH
    per_device = cols // HEAD_WIDTH
    group = devices * per_device // kv_heads
    rows = group * steps
    score_scale = 1.0 / math.sqrt(HEAD_WIDTH)
    length = len_ref[0]
    kv = recv_ref[0, :, cols:]
    for d in range(1, devices):
        kv = kv + recv_ref[d, :, cols:]
    cosine = cos_ref[...]
    sine = sin_ref[...]
    kn_s[...] = jnp.zeros_like(kn_s)
    vn_s[...] = jnp.zeros_like(vn_s)
    fresh = kn_s.shape[0]
    col_old = lax.broadcasted_iota(jnp.int32, (rows, slots), 1)
    col_new = lax.broadcasted_iota(jnp.int32, (rows, fresh), 1)
    step_new = lax.rem(lax.broadcasted_iota(jnp.int32, (rows, fresh), 0), steps)
    for copy in copies:
        copy.wait()
    for k in range(kv_heads):
        lanes = slice(k * HEAD_WIDTH, (k + 1) * HEAD_WIDTH)
        for i in range(group):
            h = k * group + i
            d, hh = h // per_device, h % per_device
            q_s[i * steps : (i + 1) * steps, :] = recv_ref[d, :, hh * HEAD_WIDTH : (hh + 1) * HEAD_WIDTH]
        query = q_s[...].astype(BF16).astype(F32)
        query = rope(query, cosine, sine).astype(BF16)
        key_now = rope(kv[:, lanes], cosine[:steps], sine[:steps]).astype(BF16).astype(F32)
        value_now = kv[:, kv_cols + k * HEAD_WIDTH : kv_cols + (k + 1) * HEAD_WIDTH].astype(BF16).astype(F32)
        ent_ref[:, lanes] = key_now
        ent_ref[:, kv_cols + k * HEAD_WIDTH : kv_cols + (k + 1) * HEAD_WIDTH] = value_now
        kn_s[:steps, :] = key_now
        vn_s[:steps, :] = value_now
        old = nt(query, k_ref[:, lanes]) * score_scale
        old = jnp.where(col_old < length, old, MASKED)
        new = nt(query, kn_s[...].astype(BF16)) * score_scale
        new = jnp.where((col_new < steps) & (col_new <= step_new), new, MASKED)
        top = jnp.maximum(jnp.max(old, axis=1, keepdims=True), jnp.max(new, axis=1, keepdims=True))
        e_old = jnp.exp(old - top)
        e_new = jnp.exp(new - top)
        total = jnp.sum(e_old, axis=1, keepdims=True) + jnp.sum(e_new, axis=1, keepdims=True)
        p_old = (e_old / total).astype(BF16)
        p_new = (e_new / total).astype(BF16)
        out = nn(p_old, v_ref[:, lanes]) + nn(p_new, vn_s[...].astype(BF16))
        ctx_ref[k * rows : (k + 1) * rows, :] = out.astype(BF16)


def lower_kernel(at_ref, low_ref, own_ref, a_ref, b_ref, c_ref, d_ref, x_ref, rank_ref, c_s, x_s):
    lines, per_row, head = a_ref.shape
    devices = 4 * lines
    rows, cols = x_ref.shape
    steps = rows // devices
    for r, (flip, cross) in zip((a_ref, b_ref, c_ref, d_ref), KINDS):
        for k in range(lines):
            start = pl.multiple_of(piece_at(at_ref, 2 * lines, k, flip, cross) * per_row, per_row)
            c_s[pl.ds(start, per_row), :] = r[k].astype(F32)
    for h in range(per_row // steps):
        for t in range(steps):
            piece = c_s[pl.ds(h * steps + t, devices, stride=per_row), :]
            x_s[t * devices : (t + 1) * devices, h * head : (h + 1) * head] = piece.astype(BF16)
    rank_ref[...] = (nt(low_ref[...], x_s[...]).astype(BF16).astype(F32) * own_ref[...]).astype(BF16)
    start = pl.multiple_of((2 * at_ref[0] + at_ref[1]) * cols, cols)
    x_ref[...] = x_s[:, pl.ds(start, cols)]


def fetch_kernel(cross, at_ref, w_ref, dep_ref, out_ref, sems):
    chips, _, width = out_ref.shape
    core = 1 - at_ref[1] if cross else at_ref[1]
    starts = [pl.multiple_of((2 * c + core) * width, width) for c in range(chips)]
    run_copies([(w_ref.at[:, pl.ds(start, width)], out_ref.at[c]) for c, start in enumerate(starts)], sems)


def out_kernel(cross, at_ref, x_ref, w_ref, rank_ref, up_ref, o_ref):
    width = o_ref.shape[2]
    chips = w_ref.shape[0]
    core = 1 - at_ref[1] if cross else at_ref[1]
    x = x_ref[...]
    rank = rank_ref[...]
    for i in range(chips):
        dest = lax.rem(at_ref[0] + i, chips)
        lanes = pl.ds(pl.multiple_of((2 * dest + core) * width, width), width)
        o_ref[i] = nn(x, w_ref[dest]) + SCALE * tn(rank, up_ref[:, lanes])


def pair_kernel(a_ref, b_ref, *outs):
    for i, out in enumerate(outs):
        out[...] = (a_ref[i] + b_ref[i]).astype(BF16)


def total_kernel(*refs):
    total = refs[0][...].astype(F32)
    for r in refs[1:-1]:
        total = total + r[...].astype(F32)
    refs[-1][...] = total.astype(BF16)


def body(
    tokens,
    query_weight,
    key_value_weight,
    output_weight,
    cached_rotated_keys,
    cached_values,
    lengths,
    request_adapter,
    adapter_pool_slot,
    adapter_down_maps,
    query_up_maps,
    key_up_maps,
    value_up_maps,
    result_lowering_factors,
    output_up_maps,
):
    both = ("tp", "sub")
    chips = lax.axis_size("tp")
    devices = lax.axis_size(both)
    lines = chips // 2
    me = lax.axis_index(both)
    steps, requests, width = tokens.shape
    rows = steps * requests
    padded = -(-rows // 128) * 128
    cols = query_weight.shape[1]
    rank = key_up_maps.shape[1]
    assert devices == 2 * chips and chips % 2 == 0
    assert adapter_down_maps.shape[0] == 1 and requests == devices and cached_values.shape[0] == 1
    at = jnp.stack([lax.axis_index("tp"), lax.axis_index("sub")]).astype(jnp.int32)

    def swap_core(v):
        return lax.ppermute(v, "sub", [(0, 1), (1, 0)])

    def swap_y(v):
        return lax.ppermute(v, "tp", [(i, i ^ 1) for i in range(chips)])

    def shift_chip(v, k):
        if k == 0:
            return v
        return lax.ppermute(v, "tp", [(i, (i + k) % chips) for i in range(chips)])

    def exchange(v):
        return lax.all_to_all(v, both, 0, 0, tiled=True)

    def gather(pieces, first, second):
        line = stack(pieces, *first)
        across = swap_y(line)
        across = pl.pallas_call(
            pass_kernel,
            out_shape=jax.ShapeDtypeStruct(across.shape, across.dtype),
            in_specs=[VMEM, ANY],
            compiler_params=PARAMS,
        )(across, second(line))
        return line, across, swap_core(line), swap_core(across)

    x = tokens.reshape(rows, width)
    pieces = [shift_chip(x, 2 * k) for k in range(lines)]
    ups = exchange(
        pl.pallas_call(
            split_kernel,
            out_shape=jax.ShapeDtypeStruct((devices, rank, cols), BF16),
            in_specs=[VMEM, ANY],
            compiler_params=PARAMS,
        )(query_up_maps[0], pieces[1])
    )
    gathered = gather(pieces, (), lambda line: ups)
    (down,) = ahead(ups, adapter_down_maps[0])

    index = jnp.arange(devices, dtype=jnp.int32)
    slot = jnp.sum(
        jnp.where(request_adapter[:, None] == index[None, :], adapter_pool_slot[None, :], 0), axis=1
    )
    row_slot = jnp.tile(slot, steps)[None, :]
    spread_mask = (jnp.repeat(index, rank)[:, None] == row_slot).astype(F32)
    own_mask = (row_slot == me).astype(F32)

    rank_send, rank_rest = pl.pallas_call(
        rank_kernel,
        out_shape=(
            jax.ShapeDtypeStruct((devices, rank, padded), BF16),
            jax.ShapeDtypeStruct((2 * rank, rows), BF16),
        ),
        in_specs=[SMEM] + [VMEM] * 6,
        compiler_params=PARAMS,
    )(at, down, *gathered, own_mask)
    ranks = exchange(rank_send)
    kv_width = key_value_weight.shape[1]
    query, kv = pl.pallas_call(
        query_kernel,
        out_shape=(
            jax.ShapeDtypeStruct((rows, cols), F32),
            jax.ShapeDtypeStruct((rows, kv_width), F32),
        ),
        in_specs=[SMEM] + [ANY] * 4 + [VMEM] * 6 + [ANY],
        scratch_shapes=[
            pltpu.VMEM((devices, width, cols), BF16),
            pltpu.VMEM(key_value_weight.shape, BF16),
            pltpu.VMEM(key_up_maps.shape[1:], BF16),
            pltpu.VMEM(value_up_maps.shape[1:], BF16),
            pltpu.SemaphoreType.DMA((devices,)),
            pltpu.SemaphoreType.DMA((3,)),
        ],
        compiler_params=WIDE,
    )(
        at,
        in_hbm(query_weight),
        in_hbm(key_value_weight),
        in_hbm(key_up_maps[0]),
        in_hbm(value_up_maps[0]),
        rank_rest,
        x,
        *gathered,
        rank_send,
    )
    to_rows = pl.pallas_call(
        finish_kernel,
        out_shape=jax.ShapeDtypeStruct((devices, steps, cols + kv_width), F32),
        compiler_params=PARAMS,
    )(query, kv, ranks, spread_mask, ups)
    arrived = exchange(to_rows)

    half_width = HEAD_WIDTH // 2
    frequency = ROPE_BASE ** (-2.0 * jnp.arange(half_width, dtype=F32) / HEAD_WIDTH)
    positions = lengths[0] + jnp.arange(steps, dtype=jnp.int32)
    angles = positions.astype(F32)[:, None] * frequency
    cosine, sine = jnp.cos(angles), jnp.sin(angles)
    group = 2 * devices * cols // kv_width
    heads = devices * cols // HEAD_WIDTH
    cosine = jnp.tile(jnp.concatenate([cosine, cosine], axis=1), (group, 1))
    sine = jnp.tile(jnp.concatenate([-sine, sine], axis=1), (group, 1))
    context, fresh = pl.pallas_call(
        attend_kernel,
        out_shape=(
            jax.ShapeDtypeStruct((heads * steps, HEAD_WIDTH), BF16),
            jax.ShapeDtypeStruct((steps, kv_width), F32),
        ),
        in_specs=[SMEM] + [VMEM] * 3 + [ANY] * 2,
        scratch_shapes=[
            pltpu.VMEM((group * steps, HEAD_WIDTH), F32),
            pltpu.VMEM((16, HEAD_WIDTH), F32),
            pltpu.VMEM((16, HEAD_WIDTH), F32),
            pltpu.VMEM(cached_rotated_keys.shape[1:], BF16),
            pltpu.VMEM(cached_values.shape[1:], BF16),
            pltpu.SemaphoreType.DMA((2,)),
        ],
        compiler_params=PARAMS,
    )(lengths, arrived, cosine, sine, in_hbm(cached_rotated_keys[0]), in_hbm(cached_values[0]))
    entries = fresh.astype(BF16)[:, None, :]

    def fetch(cross, after):
        return pl.pallas_call(
            functools.partial(fetch_kernel, cross),
            out_shape=jax.ShapeDtypeStruct((chips, cols, width), BF16),
            in_specs=[SMEM, ANY, ANY],
            out_specs=ANY,
            scratch_shapes=[pltpu.SemaphoreType.DMA((chips,))],
            compiler_params=PARAMS,
        )(at, in_hbm(output_weight), after)

    fetched = [fetch(True, context)]

    def fetch_rest(line):
        fetched.append(fetch(False, line))
        return fetched[1]

    contexts = gather([shift_chip(context, 2 * k) for k in range(lines)], fetched[:1], fetch_rest)
    lhs, out_rank = pl.pallas_call(
        lower_kernel,
        out_shape=(
            jax.ShapeDtypeStruct((rows, cols), BF16),
            jax.ShapeDtypeStruct((rank, rows), BF16),
        ),
        in_specs=[SMEM] + [VMEM] * 6,
        scratch_shapes=[
            pltpu.VMEM((devices * heads * steps, HEAD_WIDTH), F32),
            pltpu.VMEM((rows, heads * HEAD_WIDTH), BF16),
        ],
        compiler_params=PARAMS,
    )(at, result_lowering_factors[0], own_mask, *contexts)

    def out_half(cross):
        return pl.pallas_call(
            functools.partial(out_kernel, cross),
            out_shape=jax.ShapeDtypeStruct((chips, rows, width), F32),
            in_specs=[SMEM] + [VMEM] * 4,
            compiler_params=PARAMS,
        )(at, lhs, fetched[0 if cross else 1], out_rank, output_up_maps[0])

    received = swap_core(out_half(True))
    chip_totals = pl.pallas_call(
        pair_kernel,
        out_shape=[jax.ShapeDtypeStruct((rows, width), BF16)] * chips,
        compiler_params=PARAMS,
    )(out_half(False), received)
    final = [shift_chip(v, k) for k, v in enumerate(chip_totals)]
    attended = pl.pallas_call(
        total_kernel,
        out_shape=jax.ShapeDtypeStruct((rows, width), BF16),
        compiler_params=PARAMS,
    )(*final)
    return attended.reshape(steps, requests, width), entries


def solution(mesh):
    placed = (
        P(None, "groups", ("tp", "sub")),
        P(None, ("tp", "sub")),
        P(("tp", "sub"), None),
        P(("tp", "sub"), None),
        P(("groups", "tp", "sub"), None, None),
        P(("groups", "tp", "sub"), None, None),
        P(("groups", "tp", "sub")),
        P("groups"),
        P(),
        P(("tp", "sub"), None, None),
        P(("tp", "sub"), None, None),
        P(("tp", "sub"), None, None),
        P(("tp", "sub"), None, None),
        P(("tp", "sub"), None, None),
        P(("tp", "sub"), None, None),
    )
    return jax.shard_map(
        body,
        mesh=mesh,
        in_specs=placed,
        out_specs=(P(None, "groups", ("tp", "sub")), P(None, ("groups", "tp", "sub"), None)),
        check_vma=False,
    )
```
